32 devices in a mesh: groups: 2 (over y), ep: 16 (over z, x, core).
Axes of the slice: x: 2, y: 2, z: 4, core: 2. Of those that a mesh axis runs over, the one named last changes fastest.
Arguments:
- tokens: bfloat16 [2048, 2880], P(('groups', 'ep')), parts along dimension 0, may hold values from -6 to 6
- expert_ids: int32 [2048, 4], P(('groups', 'ep')), parts along dimension 0, may hold values from 0 to 15, all different within a row; in each aligned block of 64 rows (0 to 63, 64 to 127, ...) at most 18 rows name the same one
- gate_ints: int32 [2048, 4], P(('groups', 'ep')), parts along dimension 0, may hold values from 1 to 255
- norm_gain: float32 [2880], replicated, may hold values from 0.5 to 2
- weight_in: bfloat16 [16, 2880, 5760], P('ep'), may hold values from -0.109375 to 0.109375
- bias_in: float32 [16, 5760], P('ep'), may hold values from -3 to 3
- weight_out: bfloat16 [16, 2880, 2880], P('ep'), may hold values from -0.109375 to 0.109375
- bias_out: float32 [16, 2880], replicated, may hold values from -3 to 3
Outputs:
- mixed: bfloat16 [2048, 2880], P(('groups', 'ep')), parts along dimension 0
The draws below stay inside these ranges and needn't reach their ends.
There are 2 independent parts, one for each index of `groups`. The reference program is written for one: setup_inputs(seed, part) draws one part's arguments, and reference() takes and returns one part's arrays. A program takes and returns all parts, laid end to end along the dimension named above; an argument that names none is the same for every part. Nothing has to cross between parts.
Inputs may be any that keep to these rules, and one draw needn't show every extreme that they name: `expert_ids`: each row names 4 different experts. Within the rows of one device (aligned blocks of 64 rows) no expert is named more than 18 times.
All inputs are finite; a program needn't handle non-finite values.
Results may differ from the reference program's by a relative error of at most 0.0065.
Values may be sent and summed in bfloat16 or wider, within the bound.
No kernel may reach another device: no remote copies, remote signals or barrier semaphores. Data moves between devices by JAX's collectives and lax.ppermute only.
A program may use at most 256 MiB of HBM per device.

```python
import math
import jax
import jax.numpy as jnp
import numpy as np
from jax import lax

D = 2880
FF = 2880
EXPERTS = 16
TOPK = 4
ROWS_DEV = 64
CAP = 18
PARTS_SIZE = 1
PART_FF = 2880
ROWS = 1024
N_EP = 16


def touch_ends(result, stream_key, smallest, top_value):
    shape = result.shape
    place = [jax.random.randint(jax.random.fold_in(stream_key, axis), (), 0, shape[axis]) for axis in range(len(shape))]
    result = result.at[tuple(place)].set(smallest)
    longest = shape.index(max(shape))
    place[longest] = (place[longest] + 1) % shape[longest]
    return result.at[tuple(place)].set(top_value)


def block_levels(stream_key, dims, split, least, high):
    gain, own = 1.0, jax.random.fold_in(stream_key, 6)
    for axis_at, parts in split:
        heights = jnp.exp(jax.random.uniform(jax.random.fold_in(own, axis_at), (parts,), jnp.float32, least / len(split), high / len(split)))
        gain = gain * jnp.repeat(heights, dims[axis_at] // parts).reshape([-1 if axis == axis_at else 1 for axis in range(len(dims))])
    return gain


def routed_block(key, own, number, rows, amount, top, most, slope):
    sequence = jax.random.permutation(key, amount)
    packed, common = portions_of(amount, rows * top, most, slope, True), portions_of(amount, rows * top, most, slope, False)
    places = jnp.arange(amount)

    def named(tallies, rotation):
        used = int((tallies > 0).sum())
        fixed = max(1, used // 4)
        shifted = fixed + (places - fixed + rotation * (used - fixed)) % max(1, amount - fixed)
        return jnp.zeros((amount,), jnp.int32).at[sequence[jnp.where(places < fixed, places, shifted)]].set(jnp.asarray(tallies, jnp.int32))

    tallies = jnp.where(number % 4 == 0, named(packed, number // 4), named(common, number - number // 4 - 1))
    mixed = jax.random.permutation(jax.random.fold_in(own, 3), amount)
    source_of, sink = mixed[0:amount // 2 * 2:2], mixed[1:amount // 2 * 2:2]
    slack = jnp.minimum(tallies[source_of] - 1, most - tallies[sink]) // 2
    slack = jnp.where((source_of == sequence[0]) | (sink == sequence[0]) | (tallies[sink] == 0), 0, jnp.maximum(slack, 0))
    shifted = jax.random.randint(jax.random.fold_in(own, 4), (amount // 2,), 0, 1 << 20) % (slack + 1)
    tallies = tallies.at[source_of].add(-shifted).at[sink].add(shifted)
    labels = jnp.searchsorted(jnp.cumsum(tallies), jnp.arange(rows * top), side="right").astype(jnp.int32)
    table = labels.reshape(top, rows).T
    table = table[jax.random.permutation(jax.random.fold_in(own, 1), rows)]
    rotation = jax.random.randint(jax.random.fold_in(own, 2), (rows, 1), 0, top)
    return jnp.take_along_axis(table, (jnp.arange(top)[None, :] + rotation) % top, axis=1)


def portions_of(number_of, total, bound, skew, full):
    loads = [(1 << 20) // math.isqrt(grade ** skew) + 1 for grade in range(1, number_of + 1)]
    largest = bound if full else min(bound, max(-(-total // number_of), total * loads[0] // sum(loads)))
    least = 1 if total - largest >= number_of - 1 else 0
    given, surplus = [largest] + [least] * (number_of - 1), total - largest - least * (number_of - 1)
    while surplus > 0:
        candidates = [i for i in range(1, number_of) if given[i] < largest] or [i for i in range(1, number_of) if given[i] < bound]
        mass, left = sum([loads[i] for i in candidates]), surplus
        for i in candidates:
            extra = min(bound - given[i], max(1, left * loads[i] // mass), surplus)
            given[i] = given[i] + extra
            surplus = surplus - extra
    return np.array(given)


def gaussian(rng, extent, scale, reach, pieces=(), held_as=jnp.bfloat16):
    gain = block_levels(rng, extent, pieces, -0.22, 0.18) if pieces else 1.0
    array = jax.random.normal(rng, extent, jnp.float32) * scale * gain
    return jnp.minimum(jnp.maximum(array, -reach), reach).astype(held_as)


def setup_inputs(seed: int = 0, part: int = 0) -> dict:
    key_of = jax.random.split(jax.random.key(seed), 9)
    part_keys = jax.random.split(jax.random.fold_in(key_of[8], part), 9)
    tokens = gaussian(part_keys[0], (ROWS, D), 1.0, 6.0, ((0, 16),))
    expert_ids_keys = jax.random.split(jax.random.fold_in(part_keys[1], 1), ROWS // ROWS_DEV)
    expert_ids_turns = jax.random.permutation(jax.random.fold_in(part_keys[1], 3), ROWS // ROWS_DEV)
    expert_ids = jax.vmap(lambda own, number: routed_block(jax.random.fold_in(part_keys[1], 2), own, number, ROWS_DEV, EXPERTS, TOPK, CAP, 0))(expert_ids_keys, expert_ids_turns).reshape((ROWS, TOPK))
    gate_ints = touch_ends(jax.random.randint(part_keys[2], (ROWS, TOPK), 1, 256), jax.random.fold_in(part_keys[2], 1), 1, 255).astype(jnp.int32)
    norm_gain = jnp.clip(jnp.exp(jax.random.uniform(key_of[3], (D,), jnp.float32, math.log(0.5), math.log(2.0))), 0.5, 2.0)
    weight_in = gaussian(key_of[4], (EXPERTS * PARTS_SIZE, D, 2 * PART_FF), D ** -0.5, 0.109375, ((0, 16),))
    bias_in = gaussian(key_of[5], (EXPERTS * PARTS_SIZE, 2 * PART_FF), 0.5, 3.0, ((0, 16),), jnp.float32)
    weight_out = gaussian(key_of[6], (EXPERTS * PARTS_SIZE, PART_FF, D), FF ** -0.5, 0.109375, ((0, 16),))
    bias_out = gaussian(key_of[7], (EXPERTS, D), 0.5, 3.0, (), jnp.float32)
    return dict(tokens=tokens, expert_ids=expert_ids, gate_ints=gate_ints, norm_gain=norm_gain, weight_in=weight_in, bias_in=bias_in, weight_out=weight_out, bias_out=bias_out)


def swish_glu(pre_act, half_width):
    gate_part = pre_act[:, :half_width]
    up_part = pre_act[:, half_width:]
    return gate_part * jax.nn.sigmoid(1.702 * gate_part) * (up_part + 1.0)

def slot_tables(expert_ids, route_weight):
    entry_count = ROWS_DEV * TOPK
    flat_ids = expert_ids.reshape(N_EP, entry_count)
    one_hot = (flat_ids[:, :, None] == jnp.arange(EXPERTS, dtype=jnp.int32)[None, None, :]).astype(jnp.int32)
    earlier = jnp.cumsum(one_hot, axis=1) - one_hot
    slot_rank = lax.optimization_barrier(jnp.sum(earlier * one_hot, axis=2))
    slot_target = flat_ids * CAP + slot_rank
    source_dev = jnp.arange(N_EP, dtype=jnp.int32)[:, None] * jnp.ones((1, entry_count), jnp.int32)
    row_index = source_dev * ROWS_DEV + jnp.arange(entry_count, dtype=jnp.int32)[None, :] // TOPK
    row_table = jnp.full((N_EP, EXPERTS * CAP), -1, jnp.int32).at[source_dev, slot_target].set(row_index)
    weight_table = jnp.zeros((N_EP, EXPERTS * CAP), jnp.float32).at[source_dev, slot_target].set(route_weight.reshape(N_EP, entry_count))
    return (row_table.reshape(N_EP, EXPERTS, CAP), weight_table.reshape(N_EP, EXPERTS, CAP))

def reference(tokens, expert_ids, gate_ints, norm_gain, weight_in, bias_in, weight_out, bias_out):
    tok_float = tokens.astype(jnp.float32)
    row_scale = lax.rsqrt(lax.optimization_barrier(jnp.mean(tok_float * tok_float, axis=1, keepdims=True)) + 1e-05)
    normed = (tok_float * row_scale * norm_gain[None, :]).astype(jnp.bfloat16)
    int_gates = gate_ints.astype(jnp.float32)
    route_weight = int_gates / lax.optimization_barrier(jnp.sum(int_gates, axis=1, keepdims=True))
    row_table, weight_table = slot_tables(expert_ids, route_weight)

    def one_expert(running, expert_index):
        row_list = lax.dynamic_index_in_dim(row_table, expert_index, 1, keepdims=False).reshape(N_EP * CAP)
        slot_weight = lax.dynamic_index_in_dim(weight_table, expert_index, 1, keepdims=False).reshape(N_EP * CAP)
        safe_rows = jnp.maximum(row_list, 0)
        picked_rows = normed[safe_rows]
        part_sum = jnp.zeros((N_EP * CAP, D), jnp.float32)
        for part_index in range(PARTS_SIZE):
            weight_index = expert_index * PARTS_SIZE + part_index
            w_first = lax.dynamic_index_in_dim(weight_in, weight_index, 0, keepdims=False)
            b_first = lax.dynamic_index_in_dim(bias_in, weight_index, 0, keepdims=False)
            pre_act = jnp.dot(picked_rows, w_first, preferred_element_type=jnp.float32) + b_first[None, :]
            activated = swish_glu(pre_act, PART_FF).astype(jnp.bfloat16)
            w_second = lax.dynamic_index_in_dim(weight_out, weight_index, 0, keepdims=False)
            partial_value = jnp.dot(activated, w_second, preferred_element_type=jnp.float32).astype(jnp.bfloat16)
            part_sum = part_sum + partial_value.astype(jnp.float32)
        weighted = slot_weight[:, None] * part_sum
        running = running.at[safe_rows].add(weighted)
        return (running, None)
    running, _ = lax.scan(one_expert, jnp.zeros((ROWS, D), jnp.float32), jnp.arange(EXPERTS, dtype=jnp.int32))
    expert_hot = expert_ids[:, :, None] == jnp.arange(EXPERTS, dtype=jnp.int32)[None, None, :]
    expert_weight = lax.optimization_barrier(jnp.sum(jnp.where(expert_hot, route_weight[:, :, None], 0.0), axis=1))
    bias_term = jnp.dot(expert_weight, bias_out, precision=lax.Precision.HIGHEST)
    return (tok_float + running + bias_term).astype(jnp.bfloat16)
```

```python
import functools

import jax
import jax.numpy as jnp
from jax import lax
from jax.experimental import pallas as pl
from jax.experimental.pallas import tpu as pltpu
from jax.sharding import PartitionSpec as P

CAP = 18
LANES = 128
BLOCK = 768


def route_weights(gate_ints):
    int_gates = gate_ints.astype(jnp.float32)
    return int_gates / jnp.sum(int_gates, axis=1, keepdims=True)


def normalize(tokens, norm_gain):
    tok_float = tokens.astype(jnp.float32)
    row_scale = lax.rsqrt(jnp.mean(tok_float * tok_float, axis=1, keepdims=True) + 1e-05)
    return (tok_float * row_scale * norm_gain[None, :]).astype(jnp.bfloat16)


def exchange_shards(tokens, expert_ids, gate_ints, norm_gain, weight_in, bias_in, weight_out, bias_out):
    device_count = lax.axis_size("ep")
    expert_count = bias_out.shape[0]
    part_count = device_count // expert_count
    row_count, model_width = tokens.shape
    top_count = expert_ids.shape[1]
    capacity = CAP
    tok_float = tokens.astype(jnp.float32)
    normed = normalize(tokens, norm_gain)
    route_weight = route_weights(gate_ints)
    flat_ids = expert_ids.reshape(row_count * top_count)
    one_hot = (flat_ids[:, None] == jnp.arange(expert_count, dtype=jnp.int32)[None, :]).astype(jnp.int32)
    slot_rank = jnp.sum((jnp.cumsum(one_hot, axis=0) - one_hot) * one_hot, axis=1)
    slot_target = (flat_ids * capacity + slot_rank).reshape(row_count, top_count)
    slot_ids = jnp.arange(expert_count * capacity, dtype=jnp.int32)
    slot_match = slot_target[None, :, :] == slot_ids[:, None, None]
    picker = jnp.any(slot_match, axis=2).astype(jnp.bfloat16)
    placed = jnp.dot(picker, normed, preferred_element_type=jnp.float32).astype(jnp.bfloat16)
    combiner = jnp.transpose(jnp.sum(jnp.where(slot_match, route_weight[None, :, :], 0.0), axis=2))
    outgoing = jnp.broadcast_to(
        placed.reshape(expert_count, 1, capacity, model_width),
        (expert_count, part_count, capacity, model_width),
    ).reshape(device_count, capacity, model_width)
    arrived = lax.all_to_all(outgoing, "ep", split_axis=0, concat_axis=0, tiled=True)
    source_count, slot_count = arrived.shape[:2]
    flat_rows = arrived.reshape(source_count * slot_count, model_width)
    pre_act = jnp.dot(flat_rows, weight_in[0], preferred_element_type=jnp.float32) + bias_in[0][None, :]
    half_width = pre_act.shape[1] // 2
    gate_part = pre_act[:, :half_width]
    up_part = pre_act[:, half_width:]
    activated = (gate_part * jax.nn.sigmoid(1.702 * gate_part) * (up_part + 1.0)).astype(jnp.bfloat16)
    result = jnp.dot(activated, weight_out[0], preferred_element_type=jnp.float32).astype(jnp.bfloat16)
    returned = lax.all_to_all(
        result.reshape(source_count, slot_count, model_width), "ep", split_axis=0, concat_axis=0, tiled=True
    )
    part_sum = jnp.sum(
        returned.reshape(expert_count, part_count, capacity, model_width), axis=1, dtype=jnp.float32
    ).reshape(expert_count * capacity, model_width)
    moe_rows = jnp.dot(combiner, part_sum, precision=lax.Precision.HIGHEST)
    expert_hot = expert_ids[:, :, None] == jnp.arange(expert_count, dtype=jnp.int32)[None, None, :]
    expert_weight = jnp.sum(jnp.where(expert_hot, route_weight[:, :, None], 0.0), axis=1)
    bias_term = jnp.dot(expert_weight, bias_out, precision=lax.Precision.HIGHEST)
    return (tok_float + moe_rows + bias_term).astype(jnp.bfloat16)


def routing(tail, expert, top, slots):
    rows, width = tail.shape
    f32, bf16 = jnp.float32, jnp.bfloat16
    expert = expert.astype(f32)
    nt = (((1,), (1,)), ((), ()))
    sub = lax.broadcasted_iota(jnp.int32, (16, width), 0)
    lane = lax.broadcasted_iota(jnp.int32, (16, width), 1)
    pick_id = ((sub == lane) & (sub < top)).astype(f32).astype(bf16)
    pick_gate = ((sub + top == lane) & (sub < top)).astype(f32).astype(bf16)
    ids = lax.dot_general(pick_id, tail, nt, preferred_element_type=f32)
    gates = lax.dot_general(pick_gate, tail, nt, preferred_element_type=f32)
    entry = lax.broadcasted_iota(jnp.int32, ids.shape, 0)
    hit = jnp.where((ids == expert) & (entry < top), 1.0, 0.0)
    named = jnp.sum(hit, axis=0, keepdims=True)
    weight = jnp.sum(hit * gates, axis=0, keepdims=True) / jnp.sum(gates, axis=0, keepdims=True)
    first = lax.broadcasted_iota(jnp.int32, (rows, rows), 0)
    second = lax.broadcasted_iota(jnp.int32, (rows, rows), 1)
    upper = jnp.where(first <= second, 1.0, 0.0).astype(bf16)
    lower = jnp.where(first >= second, 1.0, 0.0).astype(bf16)
    named_wide = jnp.broadcast_to(named, (16, rows)).astype(bf16)
    count = jnp.dot(named_wide, upper, preferred_element_type=f32)[:1]
    slot = lax.broadcasted_iota(jnp.int32, (slots, rows), 0).astype(f32) + 1.0
    picker = jnp.where((count == slot) & (named > 0.5), 1.0, 0.0)
    slot_weight = jnp.sum(picker * weight, axis=1, keepdims=True)
    tail_float = tail.astype(f32)
    tail_lane = lax.broadcasted_iota(jnp.int32, tail.shape, 1)
    named_col = jnp.sum(jnp.where((tail_float == expert) & (tail_lane < top), 1.0, 0.0), axis=1, keepdims=True)
    count_col = jnp.dot(
        lower, jnp.broadcast_to(named_col, (rows, LANES)).astype(bf16), preferred_element_type=f32
    )[:, :1]
    slot_row = lax.broadcasted_iota(jnp.int32, (rows, slots), 1).astype(f32) + 1.0
    placer = jnp.where((count_col == slot_row) & (named_col > 0.5), 1.0, 0.0)
    return picker.astype(bf16), placer.astype(bf16), slot_weight


def expert_kernel(
    top, width, steps_in, expert_ref, near_ref, near_mate_ref, far_ref, far_mate_ref, win_ref, bin_ref, wout_ref,
    bout_ref, far_out, far_mate_out, near_out, near_mate_out, picked, pre, act, placers, weights,
):
    step = pl.program_id(0)
    f32, bf16 = jnp.float32, jnp.bfloat16
    half_rows = near_ref.shape[0]
    slots = picked.shape[0] // 2
    groups = ((near_ref, near_mate_ref), (far_ref, far_mate_ref))

    @pl.when(step == 0)
    def _():
        for g, (own, mate) in enumerate(groups):
            tail = jnp.concatenate([own[:, width:], mate[:, width:]], axis=0)
            picker, placer, slot_weight = routing(tail, expert_ref[0, 0], top, slots)
            placers[g] = placer
            weights[g] = slot_weight
            rows = jnp.dot(picker[:, :half_rows], own[:, :width], preferred_element_type=f32)
            rows += jnp.dot(picker[:, half_rows:], mate[:, :width], preferred_element_type=f32)
            picked[g * slots : (g + 1) * slots] = rows.astype(bf16)

    @pl.when(step < steps_in)
    def _():
        at = pl.multiple_of(step * BLOCK, BLOCK)
        pre[:, pl.ds(at, BLOCK)] = (
            jnp.dot(picked[...], win_ref[0], preferred_element_type=f32) + bin_ref[...]
        )

    @pl.when(step == steps_in)
    def _():
        for at in range(0, width, BLOCK):
            end = min(at + BLOCK, width)
            gate = pre[:, at:end]
            up = pre[:, width + at : width + end]
            act[:, at:end] = (gate * jax.nn.sigmoid(1.702 * gate) * (up + 1.0)).astype(bf16)

    @pl.when(step >= steps_in)
    def _():
        result = jnp.dot(act[...], wout_ref[0], preferred_element_type=f32) + bout_ref[...]
        for g, (own, mate) in enumerate(((near_out, near_mate_out), (far_out, far_mate_out))):
            part = (result[g * slots : (g + 1) * slots] * weights[g]).astype(bf16)
            spread = jnp.dot(placers[g], part, preferred_element_type=f32).astype(bf16)
            own[...] = spread[:half_rows]
            mate[...] = spread[half_rows:]


def run_expert(expert, blocks, top, weight_in, bias_in, weight_out, bias_row):
    half_rows, wide = blocks[0].shape
    width = weight_in.shape[1]
    hidden = weight_out.shape[1]
    slots = 2 * half_rows // 64 * CAP
    steps_in = pl.cdiv(2 * hidden, BLOCK)
    steps_out = pl.cdiv(width, BLOCK)
    whole = pl.BlockSpec((half_rows, wide), lambda j: (0, 0), pipeline_mode=pl.Buffered(1))
    first = lambda j: jnp.minimum(j, steps_in - 1)
    second = lambda j: jnp.maximum(j - steps_in, 0)
    out = pl.BlockSpec((half_rows, BLOCK), lambda j: (0, second(j)))
    return pl.pallas_call(
        functools.partial(expert_kernel, top, width, steps_in),
        grid=(steps_in + steps_out,),
        in_specs=[
            pl.BlockSpec(memory_space=pltpu.SMEM),
            whole, whole, whole, whole,
            pl.BlockSpec((1, width, BLOCK), lambda j: (0, 0, first(j))),
            pl.BlockSpec((1, BLOCK), lambda j: (0, first(j))),
            pl.BlockSpec((1, hidden, BLOCK), lambda j: (0, 0, second(j))),
            pl.BlockSpec((1, BLOCK), lambda j: (0, second(j))),
        ],
        out_specs=[out] * 4,
        out_shape=[jax.ShapeDtypeStruct((half_rows, width), jnp.bfloat16)] * 4,
        scratch_shapes=[
            pltpu.VMEM((2 * slots, width), jnp.bfloat16),
            pltpu.VMEM((2 * slots, steps_in * BLOCK), jnp.float32),
            pltpu.VMEM((2 * slots, hidden), jnp.bfloat16),
            pltpu.VMEM((2, 2 * half_rows, slots), jnp.bfloat16),
            pltpu.VMEM((2, slots, 1), jnp.float32),
        ],
        compiler_params=pltpu.CompilerParams(vmem_limit_bytes=48 * 2**20),
    )(expert, *blocks, weight_in, bias_in, weight_out, bias_row)


def ring_shards(tokens, expert_ids, gate_ints, norm_gain, weight_in, bias_in, weight_out, bias_out):
    device_count = lax.axis_size("ep")
    chips = device_count // 2
    reach = chips // 2
    ring = list(range(0, chips, 2)) + list(range(chips - 1, 0, -2))
    right = [(ring[i] * 2 + k, ring[(i + 1) % chips] * 2 + k) for i in range(chips) for k in range(2)]
    left = [(b, a) for a, b in right]
    mate = [(i, i ^ 1) for i in range(device_count)]
    send = lambda value, pairs: lax.ppermute(value, "ep", pairs)
    bf16, f32 = jnp.bfloat16, jnp.float32
    row_count, width = tokens.shape
    top = expert_ids.shape[1]
    half = row_count // 2
    spare = -width % LANES
    normed = normalize(tokens, norm_gain)
    block = jnp.concatenate(
        [normed, expert_ids.astype(bf16), gate_ints.astype(bf16), jnp.zeros((row_count, spare - 2 * top), bf16)],
        axis=1,
    )
    seen = {0: block}
    from_left = from_right = block
    for hop in range(1, reach):
        from_left, from_right = send(from_left, right), send(from_right, left)
        seen[-hop], seen[hop] = from_left, from_right
    low, high = send(from_left[:half], right), send(from_right[half:], left)
    near = jnp.concatenate([seen[0], seen[-1], seen[1], seen[-2]], axis=0)
    far = jnp.concatenate([seen[2], seen[-3], seen[3], low, high], axis=0)
    near_mate, far_mate = send(near, mate), send(far, mate)
    me = lax.axis_index("ep")
    bias_row = lax.dynamic_slice_in_dim(bias_out, me, 1, axis=0)
    far_sum, far_sum_mate, near_sum, near_sum_mate = run_expert(
        me.astype(jnp.int32).reshape(1, 1), (near, near_mate, far, far_mate), top, weight_in, bias_in, weight_out, bias_row
    )
    add = lambda a, b: (a.astype(f32) + b.astype(f32)).astype(bf16)
    far_sum = add(far_sum, send(far_sum_mate, mate))
    near_sum = add(near_sum, send(near_sum_mate, mate))
    cut = lambda value, i: value[i * row_count : (i + 1) * row_count]
    owed = {2: cut(far_sum, 0), -3: cut(far_sum, 1), 3: cut(far_sum, 2), 4: cut(far_sum, 3)}
    owed |= {0: cut(near_sum, 0), -1: cut(near_sum, 1), 1: cut(near_sum, 2), -2: cut(near_sum, 3)}
    up, down = send(owed[4][:half], right), send(owed[4][half:], left)
    up = jnp.concatenate([add(owed[3][:half], up), owed[3][half:]], axis=0)
    down = jnp.concatenate([owed[-3][:half], add(owed[-3][half:], down)], axis=0)
    for hop in range(reach - 2, 0, -1):
        up, down = add(owed[hop], send(up, right)), add(owed[-hop], send(down, left))
    up, down = send(up, right), send(down, left)
    moe = owed[0].astype(f32) + up.astype(f32) + down.astype(f32)
    return (tokens.astype(f32) + moe).astype(bf16)


def solution(mesh):
    ep = mesh.shape["ep"]

    def shards(*arrays):
        whole_experts = arrays[-1].shape[0] == ep and ep == 16
        return (ring_shards if whole_experts else exchange_shards)(*arrays)

    return jax.shard_map(
        shards,
        mesh=mesh,
        in_specs=(
            P(("groups", "ep"), None),
            P(("groups", "ep"), None),
            P(("groups", "ep"), None),
            P(),
            P("ep", None, None),
            P("ep", None),
            P("ep", None, None),
            P(),
        ),
        out_specs=P(("groups", "ep"), None),
        check_vma=False,
    )
```

```python
import functools

import jax
import jax.numpy as jnp
from jax import lax
from jax.experimental import pallas as pl
from jax.experimental.pallas import tpu as pltpu
from jax.sharding import PartitionSpec as P

CAP = 18
LANES = 128
BLOCK = 768


def route_weights(gate_ints):
    int_gates = gate_ints.astype(jnp.float32)
    return int_gates / jnp.sum(int_gates, axis=1, keepdims=True)


def normalize(tokens, norm_gain):
    tok_float = tokens.astype(jnp.float32)
    row_scale = lax.rsqrt(jnp.mean(tok_float * tok_float, axis=1, keepdims=True) + 1e-05)
    return (tok_float * row_scale * norm_gain[None, :]).astype(jnp.bfloat16)


def exchange_shards(tokens, expert_ids, gate_ints, norm_gain, weight_in, bias_in, weight_out, bias_out):
    device_count = lax.axis_size("ep")
    expert_count = bias_out.shape[0]
    part_count = device_count // expert_count
    row_count, model_width = tokens.shape
    top_count = expert_ids.shape[1]
    capacity = CAP
    tok_float = tokens.astype(jnp.float32)
    normed = normalize(tokens, norm_gain)
    route_weight = route_weights(gate_ints)
    flat_ids = expert_ids.reshape(row_count * top_count)
    one_hot = (flat_ids[:, None] == jnp.arange(expert_count, dtype=jnp.int32)[None, :]).astype(jnp.int32)
    slot_rank = jnp.sum((jnp.cumsum(one_hot, axis=0) - one_hot) * one_hot, axis=1)
    slot_target = (flat_ids * capacity + slot_rank).reshape(row_count, top_count)
    slot_ids = jnp.arange(expert_count * capacity, dtype=jnp.int32)
    slot_match = slot_target[None, :, :] == slot_ids[:, None, None]
    picker = jnp.any(slot_match, axis=2).astype(jnp.bfloat16)
    placed = jnp.dot(picker, normed, preferred_element_type=jnp.float32).astype(jnp.bfloat16)
    combiner = jnp.transpose(jnp.sum(jnp.where(slot_match, route_weight[None, :, :], 0.0), axis=2))
    outgoing = jnp.broadcast_to(
        placed.reshape(expert_count, 1, capacity, model_width),
        (expert_count, part_count, capacity, model_width),
    ).reshape(device_count, capacity, model_width)
    arrived = lax.all_to_all(outgoing, "ep", split_axis=0, concat_axis=0, tiled=True)
    source_count, slot_count = arrived.shape[:2]
    flat_rows = arrived.reshape(source_count * slot_count, model_width)
    pre_act = jnp.dot(flat_rows, weight_in[0], preferred_element_type=jnp.float32) + bias_in[0][None, :]
    half_width = pre_act.shape[1] // 2
    gate_part = pre_act[:, :half_width]
    up_part = pre_act[:, half_width:]
    activated = (gate_part * jax.nn.sigmoid(1.702 * gate_part) * (up_part + 1.0)).astype(jnp.bfloat16)
    result = jnp.dot(activated, weight_out[0], preferred_element_type=jnp.float32).astype(jnp.bfloat16)
    returned = lax.all_to_all(
        result.reshape(source_count, slot_count, model_width), "ep", split_axis=0, concat_axis=0, tiled=True
    )
    part_sum = jnp.sum(
        returned.reshape(expert_count, part_count, capacity, model_width), axis=1, dtype=jnp.float32
    ).reshape(expert_count * capacity, model_width)
    moe_rows = jnp.dot(combiner, part_sum, precision=lax.Precision.HIGHEST)
    expert_hot = expert_ids[:, :, None] == jnp.arange(expert_count, dtype=jnp.int32)[None, None, :]
    expert_weight = jnp.sum(jnp.where(expert_hot, route_weight[:, :, None], 0.0), axis=1)
    bias_term = jnp.dot(expert_weight, bias_out, precision=lax.Precision.HIGHEST)
    return (tok_float + moe_rows + bias_term).astype(jnp.bfloat16)


def norm_kernel(top, tokens_ref, ids_ref, gates_ref, gain_ref, *out_refs):
    f32, bf16 = jnp.float32, jnp.bfloat16
    rows, width = tokens_ref.shape
    tok = tokens_ref[...].astype(f32)
    scale = lax.rsqrt(jnp.mean(tok * tok, axis=1, keepdims=True) + 1e-05)
    normed = (tok * scale * gain_ref[...]).astype(bf16)
    spare = sum(ref.shape[1] for ref in out_refs) - width
    sub = lax.broadcasted_iota(jnp.int32, (top, spare), 0)
    lane = lax.broadcasted_iota(jnp.int32, (top, spare), 1)
    turn = (((0,), (0,)), ((), ()))
    tail = lax.dot_general(
        ids_ref[...].astype(f32), jnp.where(lane == sub, 1.0, 0.0), turn, preferred_element_type=f32
    ) + lax.dot_general(
        gates_ref[...].astype(f32), jnp.where(lane == sub + top, 1.0, 0.0), turn, preferred_element_type=f32
    )
    at = 0
    for ref in out_refs:
        end = at + ref.shape[1]
        ref[:, : min(end, width) - at] = normed[:, at : min(end, width)]
        if end > width:
            ref[:, width - at :] = tail.astype(bf16)
        at = end


def pick_kernel(top, width, counts, experts_ref, *refs):
    f32, bf16 = jnp.float32, jnp.bfloat16
    pieces, (own_out, mate_out, placer_out, held) = refs[: sum(counts)], refs[sum(counts) :]
    at_piece = lane_at = 0
    for count in counts:
        row_at = 0
        for ref in pieces[at_piece : at_piece + count]:
            rows, lanes = ref.shape
            held[row_at : row_at + rows, lane_at : lane_at + lanes] = ref[...]
            row_at += rows
        at_piece, lane_at = at_piece + count, lane_at + lanes
    tail = held[:, width:]
    slots = own_out.shape[0]
    rows = tail.shape[0]
    sub = lax.broadcasted_iota(jnp.int32, (16, tail.shape[1]), 0)
    lane = lax.broadcasted_iota(jnp.int32, (16, tail.shape[1]), 1)
    pick_id = jnp.where((sub == lane) & (sub < top), 1.0, 0.0).astype(bf16)
    ids = lax.dot_general(pick_id, tail, (((1,), (1,)), ((), ())), preferred_element_type=f32)
    entry = lax.broadcasted_iota(jnp.int32, ids.shape, 0)
    first = lax.broadcasted_iota(jnp.int32, (rows, rows), 0)
    second = lax.broadcasted_iota(jnp.int32, (rows, rows), 1)
    upper = jnp.where(first <= second, 1.0, 0.0).astype(bf16)
    lower = jnp.where(first >= second, 1.0, 0.0).astype(bf16)
    tail_float = tail.astype(f32)
    tail_lane = lax.broadcasted_iota(jnp.int32, tail.shape, 1)
    slot = lax.broadcasted_iota(jnp.int32, (slots, rows), 0).astype(f32) + 1.0
    slot_lane = lax.broadcasted_iota(jnp.int32, (rows, slots), 1).astype(f32) + 1.0
    placers = []
    for i, out in enumerate((own_out, mate_out)):
        expert = experts_ref[0, i].astype(f32)
        named = jnp.sum(jnp.where((ids == expert) & (entry < top), 1.0, 0.0), axis=0, keepdims=True)
        count = jnp.dot(jnp.broadcast_to(named, (16, rows)).astype(bf16), upper, preferred_element_type=f32)[:1]
        picker = jnp.where((count == slot) & (named > 0.5), 1.0, 0.0).astype(bf16)
        out[...] = jnp.dot(picker, held[...], preferred_element_type=f32).astype(bf16)
        named = jnp.sum(jnp.where((tail_float == expert) & (tail_lane < top), 1.0, 0.0), axis=1, keepdims=True)
        count = jnp.dot(lower, jnp.broadcast_to(named, (rows, LANES)).astype(bf16), preferred_element_type=f32)
        placers.append(jnp.where((count[:, :1] == slot_lane) & (named > 0.5), 1.0, 0.0))
    placer_out[...] = jnp.concatenate(placers, axis=1).astype(bf16)


def slot_weights(rows, width, top, expert):
    f32 = jnp.float32
    tail = rows[:, width:]
    lane = lax.broadcasted_iota(jnp.int32, tail.shape, 1)
    spare = tail.shape[1]
    first = lax.broadcasted_iota(jnp.int32, (spare, spare), 0)
    second = lax.broadcasted_iota(jnp.int32, (spare, spare), 1)
    shift = jnp.where((first == second + top) & (second < top), 1.0, 0.0).astype(jnp.bfloat16)
    gates = jnp.dot(tail, shift, preferred_element_type=f32)
    hit = (tail.astype(f32) == expert) & (lane < top)
    total = jnp.sum(gates, axis=1, keepdims=True)
    return jnp.sum(jnp.where(hit, gates, 0.0), axis=1, keepdims=True) / jnp.maximum(total, 1.0)


def expert_kernel(
    top, steps_in, experts_ref, own_ref, mate_ref, win_ref, bin_ref, wout_ref, bout_ref,
    own_out, mate_out, act_out, weight_out, picked, pre,
):
    step = pl.program_id(0)
    f32, bf16 = jnp.float32, jnp.bfloat16
    slots, hidden, width = own_ref.shape[0], act_out.shape[1], picked.shape[1]

    @pl.when(step == 0)
    def _():
        picked[:slots] = own_ref[:, :width]
        picked[slots:] = mate_ref[:, :width]
        expert = experts_ref[0, 0].astype(f32)
        for i, ref in enumerate((own_ref, mate_ref)):
            weight = slot_weights(ref, width, top, expert)
            weight_out[i * slots : (i + 1) * slots] = jnp.broadcast_to(weight, (slots, LANES))

    @pl.when(step < steps_in)
    def _():
        at = pl.multiple_of(step * BLOCK, BLOCK)
        pre[:, pl.ds(at, BLOCK)] = jnp.dot(picked[...], win_ref[0], preferred_element_type=f32) + bin_ref[...]

    @pl.when(step == steps_in)
    def _():
        for at in range(0, hidden, 256):
            end = min(at + 256, hidden)
            gate = pre[:, at:end]
            up = pre[:, hidden + at : hidden + end]
            act_out[:, at:end] = (gate * jax.nn.sigmoid(1.702 * gate) * (up + 1.0)).astype(bf16)

    @pl.when(step >= steps_in)
    def _():
        result = jnp.dot(act_out[...], wout_ref[0], preferred_element_type=f32) + bout_ref[...]
        result = (result * weight_out[:, :1]).astype(bf16)
        own_out[...] = result[:slots]
        mate_out[...] = result[slots:]


def second_kernel(act_ref, weight_ref, wout_ref, bout_ref, own_out, mate_out):
    slots = own_out.shape[0]
    result = jnp.dot(act_ref[...], wout_ref[0], preferred_element_type=jnp.float32) + bout_ref[...]
    result = (result * weight_ref[:, :1]).astype(jnp.bfloat16)
    own_out[...] = result[:slots]
    mate_out[...] = result[slots:]


def spread_kernel(placer_ref, own_ref, mate_ref, *out_refs):
    slots = own_ref.shape[0]
    f32 = jnp.float32
    at = 0
    for ref in out_refs:
        rows = ref.shape[0]
        part = placer_ref[at : at + rows]
        total = jnp.dot(part[:, :slots], own_ref[...], preferred_element_type=f32)
        total += jnp.dot(part[:, slots:], mate_ref[...], preferred_element_type=f32)
        ref[...] = total.astype(ref.dtype)
        at += rows


def params(mib):
    return pltpu.CompilerParams(vmem_limit_bytes=mib * 2**20)


def ring_shards(tokens, expert_ids, gate_ints, norm_gain, weight_in, bias_in, weight_out, bias_out):
    device_count = lax.axis_size("ep")
    chips = device_count // 2
    reach = chips // 2
    ring = list(range(0, chips, 2)) + list(range(chips - 1, 0, -2))
    right = [(ring[i] * 2 + k, ring[(i + 1) % chips] * 2 + k) for i in range(chips) for k in range(2)]
    left = [(b, a) for a, b in right]
    mate = [(i, i ^ 1) for i in range(device_count)]
    send = lambda value, pairs: lax.ppermute(value, "ep", pairs)
    bf16, f32 = jnp.bfloat16, jnp.float32
    row_count, width = tokens.shape
    top = expert_ids.shape[1]
    hidden = weight_out.shape[1]
    half = row_count // 2
    wide = width + -width % LANES
    lanes = [2 * BLOCK, wide - 2 * BLOCK]
    slots = chips * CAP
    vmem = pl.BlockSpec(memory_space=pltpu.VMEM)
    smem = pl.BlockSpec(memory_space=pltpu.SMEM)
    shape = lambda rows, cols, dtype=bf16: jax.ShapeDtypeStruct((rows, cols), dtype)

    chains = pl.pallas_call(
        functools.partial(norm_kernel, top),
        in_specs=[vmem] * 4,
        out_specs=[vmem] * 2,
        out_shape=[shape(row_count, w) for w in lanes],
        compiler_params=params(16),
    )(tokens, expert_ids.T, gate_ints.T, norm_gain[None, :])
    me = lax.axis_index("ep").astype(jnp.int32)
    experts = jnp.stack([me, me ^ 1]).reshape(1, 2)
    bias_row = lax.dynamic_slice_in_dim(bias_out, me, 1, axis=0)

    held = [[chain] for chain in chains]
    going = [(chain, chain) for chain in chains]
    for hop in range(1, reach + 1):
        for c in range(len(chains)):
            to_right, to_left = going[c]
            if hop == reach:
                to_right, to_left = to_right[:half], to_left[half:]
            going[c] = send(to_right, right), send(to_left, left)
            held[c] += going[c]
    order = [0]
    for hop in range(1, reach):
        order += [-hop, hop]
    pieces = held[0] + held[1]
    picked, picked_mate, placer = pl.pallas_call(
        functools.partial(pick_kernel, top, width, [len(h) for h in held]),
        in_specs=[smem] + [vmem] * len(pieces),
        out_specs=[vmem] * 3,
        out_shape=[shape(slots, wide), shape(slots, wide), shape(chips * row_count, 2 * slots)],
        scratch_shapes=[pltpu.VMEM((chips * row_count, wide), bf16)],
        compiler_params=params(24),
    )(experts, *pieces)
    picked_mate = send(picked_mate, mate)

    steps_in = pl.cdiv(2 * hidden, BLOCK)
    steps_a = lanes[0] // BLOCK
    steps_b = pl.cdiv(width - lanes[0], BLOCK)
    first = lambda j: jnp.minimum(j, steps_in - 1)
    second = lambda j: jnp.maximum(j - steps_in, 0)
    whole = lambda rows, cols: pl.BlockSpec((rows, cols), lambda j: (0, 0), pipeline_mode=pl.Buffered(1))
    own_a, mate_a, act, slot_weight = pl.pallas_call(
        functools.partial(expert_kernel, top, steps_in),
        grid=(steps_in + steps_a,),
        in_specs=[
            smem, whole(slots, wide), whole(slots, wide),
            pl.BlockSpec((1, width, BLOCK), lambda j: (0, 0, first(j))),
            pl.BlockSpec((1, BLOCK), lambda j: (0, first(j))),
            pl.BlockSpec((1, hidden, BLOCK), lambda j: (0, 0, second(j))),
            pl.BlockSpec((1, BLOCK), lambda j: (0, second(j))),
        ],
        out_specs=[pl.BlockSpec((slots, BLOCK), lambda j: (0, second(j)))] * 2
        + [whole(2 * slots, hidden), whole(2 * slots, LANES)],
        out_shape=[shape(slots, lanes[0])] * 2 + [shape(2 * slots, hidden), shape(2 * slots, LANES, f32)],
        scratch_shapes=[
            pltpu.VMEM((2 * slots, width), bf16),
            pltpu.VMEM((2 * slots, steps_in * BLOCK), f32),
        ],
        compiler_params=params(40),
    )(experts, picked, picked_mate, weight_in, bias_in, weight_out, bias_row)
    own_b, mate_b = pl.pallas_call(
        second_kernel,
        grid=(steps_b,),
        in_specs=[
            whole(2 * slots, hidden), whole(2 * slots, LANES),
            pl.BlockSpec((1, hidden, BLOCK), lambda j: (0, 0, j + steps_a)),
            pl.BlockSpec((1, BLOCK), lambda j: (0, j + steps_a)),
        ],
        out_specs=[pl.BlockSpec((slots, BLOCK), lambda j: (0, j))] * 2,
        out_shape=[shape(slots, lanes[1])] * 2,
        compiler_params=params(24),
    )(act, slot_weight, weight_out, bias_row)

    heights = [row_count] * (chips - 1) + [half, half]
    add = lambda a, b: (a.astype(f32) + b.astype(f32)).astype(bf16)
    owed = []
    for own, other in ((own_a, mate_a), (own_b, mate_b)):
        sums = pl.pallas_call(
            spread_kernel,
            in_specs=[vmem] * 3,
            out_specs=[vmem] * len(heights),
            out_shape=[shape(rows, own.shape[1]) for rows in heights],
            compiler_params=params(16),
        )(placer, own, send(other, mate))
        owed.append(dict(zip(order + ["right", "left"], sums)))
    going = [(o["right"], o["left"]) for o in owed]
    for hop in range(reach - 1, -1, -1):
        for c in range(len(owed)):
            up, down = send(going[c][0], right), send(going[c][1], left)
            if hop == reach - 1:
                ahead, behind = owed[c][hop], owed[c][-hop]
                up = jnp.concatenate([add(ahead[:half], up), ahead[half:]], axis=0)
                down = jnp.concatenate([behind[:half], add(behind[half:], down)], axis=0)
            elif hop:
                up, down = add(owed[c][hop], up), add(owed[c][-hop], down)
            going[c] = up, down
    moe = [o[0].astype(f32) + up.astype(f32) + down.astype(f32) for o, (up, down) in zip(owed, going)]
    return (tokens.astype(f32) + jnp.concatenate(moe, axis=1)[:, :width]).astype(bf16)


def solution(mesh):
    ep = mesh.shape["ep"]

    def shards(*arrays):
        whole_experts = arrays[-1].shape[0] == ep and ep == 16
        return (ring_shards if whole_experts else exchange_shards)(*arrays)

    return jax.shard_map(
        shards,
        mesh=mesh,
        in_specs=(
            P(("groups", "ep"), None),
            P(("groups", "ep"), None),
            P(("groups", "ep"), None),
            P(),
            P("ep", None, None),
            P("ep", None),
            P("ep", None, None),
            P(),
        ),
        out_specs=P(("groups", "ep"), None),
        check_vma=False,
    )
```

```python
import functools

import jax
import jax.numpy as jnp
from jax import lax
from jax.experimental import pallas as pl
from jax.experimental.pallas import tpu as pltpu
from jax.sharding import PartitionSpec as P

CAP = 18
LANES = 128
BLOCK = 768
NORM_MIB = 16
SMALL_MIB = 16
EXPERT_MIB = 44


def route_weights(gate_ints):
    int_gates = gate_ints.astype(jnp.float32)
    return int_gates / jnp.sum(int_gates, axis=1, keepdims=True)


def normalize(tokens, norm_gain):
    tok_float = tokens.astype(jnp.float32)
    row_scale = lax.rsqrt(jnp.mean(tok_float * tok_float, axis=1, keepdims=True) + 1e-05)
    return (tok_float * row_scale * norm_gain[None, :]).astype(jnp.bfloat16)


def exchange_shards(tokens, expert_ids, gate_ints, norm_gain, weight_in, bias_in, weight_out, bias_out):
    device_count = lax.axis_size("ep")
    expert_count = bias_out.shape[0]
    part_count = device_count // expert_count
    row_count, model_width = tokens.shape
    top_count = expert_ids.shape[1]
    capacity = CAP
    tok_float = tokens.astype(jnp.float32)
    normed = normalize(tokens, norm_gain)
    route_weight = route_weights(gate_ints)
    flat_ids = expert_ids.reshape(row_count * top_count)
    one_hot = (flat_ids[:, None] == jnp.arange(expert_count, dtype=jnp.int32)[None, :]).astype(jnp.int32)
    slot_rank = jnp.sum((jnp.cumsum(one_hot, axis=0) - one_hot) * one_hot, axis=1)
    slot_target = (flat_ids * capacity + slot_rank).reshape(row_count, top_count)
    slot_ids = jnp.arange(expert_count * capacity, dtype=jnp.int32)
    slot_match = slot_target[None, :, :] == slot_ids[:, None, None]
    picker = jnp.any(slot_match, axis=2).astype(jnp.bfloat16)
    placed = jnp.dot(picker, normed, preferred_element_type=jnp.float32).astype(jnp.bfloat16)
    combiner = jnp.transpose(jnp.sum(jnp.where(slot_match, route_weight[None, :, :], 0.0), axis=2))
    outgoing = jnp.broadcast_to(
        placed.reshape(expert_count, 1, capacity, model_width),
        (expert_count, part_count, capacity, model_width),
    ).reshape(device_count, capacity, model_width)
    arrived = lax.all_to_all(outgoing, "ep", split_axis=0, concat_axis=0, tiled=True)
    source_count, slot_count = arrived.shape[:2]
    flat_rows = arrived.reshape(source_count * slot_count, model_width)
    pre_act = jnp.dot(flat_rows, weight_in[0], preferred_element_type=jnp.float32) + bias_in[0][None, :]
    half_width = pre_act.shape[1] // 2
    gate_part = pre_act[:, :half_width]
    up_part = pre_act[:, half_width:]
    activated = (gate_part * jax.nn.sigmoid(1.702 * gate_part) * (up_part + 1.0)).astype(jnp.bfloat16)
    result = jnp.dot(activated, weight_out[0], preferred_element_type=jnp.float32).astype(jnp.bfloat16)
    returned = lax.all_to_all(
        result.reshape(source_count, slot_count, model_width), "ep", split_axis=0, concat_axis=0, tiled=True
    )
    part_sum = jnp.sum(
        returned.reshape(expert_count, part_count, capacity, model_width), axis=1, dtype=jnp.float32
    ).reshape(expert_count * capacity, model_width)
    moe_rows = jnp.dot(combiner, part_sum, precision=lax.Precision.HIGHEST)
    expert_hot = expert_ids[:, :, None] == jnp.arange(expert_count, dtype=jnp.int32)[None, None, :]
    expert_weight = jnp.sum(jnp.where(expert_hot, route_weight[:, :, None], 0.0), axis=1)
    bias_term = jnp.dot(expert_weight, bias_out, precision=lax.Precision.HIGHEST)
    return (tok_float + moe_rows + bias_term).astype(jnp.bfloat16)


def norm_kernel(top, tokens_ref, ids_ref, gates_ref, gain_ref, first_ref, second_ref):
    f32, bf16 = jnp.float32, jnp.bfloat16
    tok = tokens_ref[...].astype(f32)
    scale = lax.rsqrt(jnp.mean(tok * tok, axis=1, keepdims=True) + 1e-05)
    normed = (tok * scale * gain_ref[...][None, :]).astype(bf16)
    cut = tok.shape[1] - second_ref.shape[1]
    spare = first_ref.shape[1] - cut
    sub = lax.broadcasted_iota(jnp.int32, (top, spare), 0)
    lane = lax.broadcasted_iota(jnp.int32, (top, spare), 1)
    turn = (((0,), (0,)), ((), ()))
    tail = lax.dot_general(
        ids_ref[...].astype(f32), jnp.where(lane == sub, 1.0, 0.0), turn, preferred_element_type=f32
    ) + lax.dot_general(
        gates_ref[...].astype(f32), jnp.where(lane == sub + top, 1.0, 0.0), turn, preferred_element_type=f32
    )
    first_ref[:, :cut] = normed[:, :cut]
    first_ref[:, cut:] = tail.astype(bf16)
    second_ref[...] = normed[:, cut:]


def gather_rows(pieces, held):
    at = 0
    for ref in pieces:
        held[at : at + ref.shape[0]] = ref[...]
        at += ref.shape[0]


def route_kernel(top, cut, count, experts_ref, *refs):
    f32, bf16 = jnp.float32, jnp.bfloat16
    own_out, mate_out, picker_out, placer_out, held = refs[count:]
    gather_rows(refs[:count], held)
    tail = held[:, cut:]
    slots = own_out.shape[0]
    rows = tail.shape[0]
    sub = lax.broadcasted_iota(jnp.int32, (16, tail.shape[1]), 0)
    lane = lax.broadcasted_iota(jnp.int32, (16, tail.shape[1]), 1)
    pick_id = jnp.where((sub == lane) & (sub < top), 1.0, 0.0).astype(bf16)
    ids = lax.dot_general(pick_id, tail, (((1,), (1,)), ((), ())), preferred_element_type=f32)
    entry = lax.broadcasted_iota(jnp.int32, ids.shape, 0)
    first = lax.broadcasted_iota(jnp.int32, (rows, rows), 0)
    second = lax.broadcasted_iota(jnp.int32, (rows, rows), 1)
    upper = jnp.where(first <= second, 1.0, 0.0).astype(bf16)
    lower = jnp.where(first >= second, 1.0, 0.0).astype(bf16)
    tail_float = tail.astype(f32)
    tail_lane = lax.broadcasted_iota(jnp.int32, tail.shape, 1)
    slot = lax.broadcasted_iota(jnp.int32, (slots, rows), 0).astype(f32) + 1.0
    slot_lane = lax.broadcasted_iota(jnp.int32, (rows, slots), 1).astype(f32) + 1.0
    placers = []
    for i, out in enumerate((own_out, mate_out)):
        expert = experts_ref[0, i].astype(f32)
        named = jnp.sum(jnp.where((ids == expert) & (entry < top), 1.0, 0.0), axis=0, keepdims=True)
        number = jnp.dot(jnp.broadcast_to(named, (16, rows)).astype(bf16), upper, preferred_element_type=f32)[:1]
        picker = jnp.where((number == slot) & (named > 0.5), 1.0, 0.0).astype(bf16)
        picker_out[i * slots : (i + 1) * slots] = picker
        out[...] = jnp.dot(picker, held[...], preferred_element_type=f32).astype(bf16)
        named = jnp.sum(jnp.where((tail_float == expert) & (tail_lane < top), 1.0, 0.0), axis=1, keepdims=True)
        number = jnp.dot(lower, jnp.broadcast_to(named, (rows, LANES)).astype(bf16), preferred_element_type=f32)
        placers.append(jnp.where((number[:, :1] == slot_lane) & (named > 0.5), 1.0, 0.0))
    placer_out[...] = jnp.concatenate(placers, axis=1).astype(bf16)


def pick_kernel(count, picker_ref, *refs):
    own_out, mate_out, held = refs[count:]
    gather_rows(refs[:count], held)
    rows = jnp.dot(picker_ref[...], held[...], preferred_element_type=jnp.float32).astype(jnp.bfloat16)
    slots = own_out.shape[0]
    own_out[...] = rows[:slots]
    mate_out[...] = rows[slots:]


def slot_weights(tail, top, expert):
    f32 = jnp.float32
    lane = lax.broadcasted_iota(jnp.int32, tail.shape, 1)
    spare = tail.shape[1]
    first = lax.broadcasted_iota(jnp.int32, (spare, spare), 0)
    second = lax.broadcasted_iota(jnp.int32, (spare, spare), 1)
    shift = jnp.where((first == second + top) & (second < top), 1.0, 0.0).astype(jnp.bfloat16)
    gates = jnp.dot(tail, shift, preferred_element_type=f32)
    hit = (tail.astype(f32) == expert) & (lane < top)
    total = jnp.sum(gates, axis=1, keepdims=True)
    return jnp.sum(jnp.where(hit, gates, 0.0), axis=1, keepdims=True) / jnp.maximum(total, 1.0)


def expert_kernel(
    top, steps_in, steps_a, experts_ref, own_first, mate_first, own_second, mate_second, win_ref, bin_ref, wout_ref,
    bout_ref, own_a, mate_a, own_b, mate_b, rows_first, rows_second, pre, act, slot_weight,
):
    step = pl.program_id(0)
    f32, bf16 = jnp.float32, jnp.bfloat16
    slots, hidden = own_first.shape[0], act.shape[1]
    cut = win_ref.shape[1] - own_second.shape[1]

    @pl.when(step == 0)
    def _():
        expert = experts_ref[0, 0].astype(f32)
        for i, (low, high) in enumerate(((own_first, own_second), (mate_first, mate_second))):
            rows_first[i * slots : (i + 1) * slots] = low[...]
            rows_second[i * slots : (i + 1) * slots] = high[...]
            weight = slot_weights(low[:, cut:], top, expert)
            slot_weight[i * slots : (i + 1) * slots] = jnp.broadcast_to(weight, (slots, LANES))

    @pl.when(step < steps_in)
    def _():
        at = pl.multiple_of(step * BLOCK, BLOCK)
        total = jnp.dot(rows_first[:, :cut], win_ref[0, :cut], preferred_element_type=f32)
        total += jnp.dot(rows_second[...], win_ref[0, cut:], preferred_element_type=f32)
        pre[:, pl.ds(at, BLOCK)] = total + bin_ref[...]

    @pl.when(step == steps_in)
    def _():
        for at in range(0, hidden, 256):
            end = min(at + 256, hidden)
            gate = pre[:, at:end]
            up = pre[:, hidden + at : hidden + end]
            act[:, at:end] = (gate * jax.nn.sigmoid(1.702 * gate) * (up + 1.0)).astype(bf16)

    @pl.when(step >= steps_in)
    def _():
        result = jnp.dot(act[...], wout_ref[0], preferred_element_type=f32) + bout_ref[...]
        result = (result * slot_weight[:, :1]).astype(bf16)

        @pl.when(step < steps_in + steps_a)
        def _():
            own_a[...] = result[:slots]
            mate_a[...] = result[slots:]

        @pl.when(step >= steps_in + steps_a)
        def _():
            own_b[...] = result[:slots]
            mate_b[...] = result[slots:]


def spread_kernel(placer_ref, own_ref, mate_ref, *out_refs):
    slots = own_ref.shape[0]
    f32 = jnp.float32
    total = jnp.dot(placer_ref[:, :slots], own_ref[...], preferred_element_type=f32)
    total += jnp.dot(placer_ref[:, slots:], mate_ref[...], preferred_element_type=f32)
    at = 0
    for ref in out_refs:
        ref[...] = total[at : at + ref.shape[0]].astype(ref.dtype)
        at += ref.shape[0]


def params(mib):
    return pltpu.CompilerParams(vmem_limit_bytes=mib * 2**20)


def cost(macs, moved):
    return pl.CostEstimate(flops=2 * macs, bytes_accessed=moved, transcendentals=0)


def ring_shards(tokens, expert_ids, gate_ints, norm_gain, weight_in, bias_in, weight_out, bias_out):
    device_count = lax.axis_size("ep")
    chips = device_count // 2
    reach = chips // 2
    ring = list(range(0, chips, 2)) + list(range(chips - 1, 0, -2))
    right = [(ring[i] * 2 + k, ring[(i + 1) % chips] * 2 + k) for i in range(chips) for k in range(2)]
    left = [(b, a) for a, b in right]
    mate = [(i, i ^ 1) for i in range(device_count)]
    send = lambda value, pairs: lax.ppermute(value, "ep", pairs)
    bf16, f32 = jnp.bfloat16, jnp.float32
    row_count, width = tokens.shape
    top = expert_ids.shape[1]
    hidden = weight_out.shape[1]
    half = row_count // 2
    lanes = [2 * BLOCK, width + -width % LANES - 2 * BLOCK]
    cut = width - lanes[1]
    slots, all_rows = chips * CAP, chips * row_count
    vmem = pl.BlockSpec(memory_space=pltpu.VMEM)
    smem = pl.BlockSpec(memory_space=pltpu.SMEM)
    shape = lambda rows, cols, dtype=bf16: jax.ShapeDtypeStruct((rows, cols), dtype)

    chains = pl.pallas_call(
        functools.partial(norm_kernel, top),
        in_specs=[vmem] * 4,
        out_specs=[vmem] * 2,
        out_shape=[shape(row_count, w) for w in lanes],
        compiler_params=params(NORM_MIB),
    )(tokens, expert_ids.T, gate_ints.T, norm_gain)
    me = lax.axis_index("ep").astype(jnp.int32)
    experts = jnp.stack([me, me ^ 1]).reshape(1, 2)
    bias_row = lax.dynamic_slice_in_dim(bias_out, me, 1, axis=0)

    held = [[chain] for chain in chains]
    going = [(chain, chain) for chain in chains]
    for hop in range(1, reach + 1):
        for c in range(len(chains)):
            to_right, to_left = going[c]
            if hop == reach:
                to_right, to_left = to_right[:half], to_left[half:]
                if c:
                    to_right, to_left, _ = lax.optimization_barrier((to_right, to_left, waited))
                waited = going[c]
            going[c] = send(to_right, right), send(to_left, left)
            held[c] += going[c]
    order = [0]
    for hop in range(1, reach):
        order += [-hop, hop]
    own_first, mate_first, picker, placer = pl.pallas_call(
        functools.partial(route_kernel, top, cut, len(held[0])),
        in_specs=[smem] + [vmem] * len(held[0]),
        out_specs=[vmem] * 4,
        out_shape=[shape(slots, lanes[0])] * 2 + [shape(2 * slots, all_rows), shape(all_rows, 2 * slots)],
        scratch_shapes=[pltpu.VMEM((all_rows, lanes[0]), bf16)],
        cost_estimate=cost(2 * slots * all_rows * lanes[0], 2**20),
        compiler_params=params(SMALL_MIB),
    )(experts, *held[0])
    mate_first = send(mate_first, mate)
    own_second, mate_second = pl.pallas_call(
        functools.partial(pick_kernel, len(held[1])),
        in_specs=[vmem] * (1 + len(held[1])),
        out_specs=[vmem] * 2,
        out_shape=[shape(slots, lanes[1])] * 2,
        scratch_shapes=[pltpu.VMEM((all_rows, lanes[1]), bf16)],
        cost_estimate=cost(2 * slots * all_rows * lanes[1], 2**20),
        compiler_params=params(SMALL_MIB),
    )(picker, *held[1])
    mate_second = send(mate_second, mate)

    steps_in = pl.cdiv(2 * hidden, BLOCK)
    steps_out = pl.cdiv(width, BLOCK)
    first = lambda j: jnp.minimum(j, steps_in - 1)
    second = lambda j: jnp.maximum(j - steps_in, 0)
    whole = lambda rows, cols: pl.BlockSpec((rows, cols), lambda j: (0, 0), pipeline_mode=pl.Buffered(1))
    steps_a = lanes[0] // BLOCK
    out_a = pl.BlockSpec((slots, BLOCK), lambda j: (0, jnp.minimum(second(j), steps_a - 1)))
    out_b = pl.BlockSpec((slots, BLOCK), lambda j: (0, jnp.maximum(second(j) - steps_a, 0)))
    own_a, mate_a, own_b, mate_b = pl.pallas_call(
        functools.partial(expert_kernel, top, steps_in, steps_a),
        grid=(steps_in + steps_out,),
        in_specs=[
            smem, whole(slots, lanes[0]), whole(slots, lanes[0]), whole(slots, lanes[1]), whole(slots, lanes[1]),
            pl.BlockSpec((1, width, BLOCK), lambda j: (0, 0, first(j))),
            pl.BlockSpec((1, BLOCK), lambda j: (0, first(j))),
            pl.BlockSpec((1, hidden, BLOCK), lambda j: (0, 0, second(j))),
            pl.BlockSpec((1, BLOCK), lambda j: (0, second(j))),
        ],
        out_specs=[out_a, out_a, out_b, out_b],
        out_shape=[shape(slots, w) for w in (lanes[0], lanes[0], lanes[1], lanes[1])],
        scratch_shapes=[
            pltpu.VMEM((2 * slots, lanes[0]), bf16),
            pltpu.VMEM((2 * slots, lanes[1]), bf16),
            pltpu.VMEM((2 * slots, steps_in * BLOCK), f32),
            pltpu.VMEM((2 * slots, hidden), bf16),
            pltpu.VMEM((2 * slots, LANES), f32),
        ],
        cost_estimate=cost(2 * slots * width * 3 * hidden, 6 * width * hidden),
        compiler_params=params(EXPERT_MIB),
    )(experts, own_first, mate_first, own_second, mate_second, weight_in, bias_in, weight_out, bias_row)

    heights = [row_count] * (chips - 1) + [half, half]
    add = lambda a, b: (a.astype(f32) + b.astype(f32)).astype(bf16)

    def spread(own, other):
        sums = pl.pallas_call(
            spread_kernel,
            in_specs=[vmem] * 3,
            out_specs=[vmem] * len(heights),
            out_shape=[shape(rows, own.shape[1]) for rows in heights],
            cost_estimate=cost(2 * slots * all_rows * own.shape[1], 2**20),
            compiler_params=params(SMALL_MIB),
        )(placer, own, send(other, mate))
        return dict(zip(order + ["right", "left"], sums))

    owed = [spread(own_a, mate_a), spread(own_b, mate_b)]
    going = [(o["right"], o["left"]) for o in owed]
    for hop in range(reach - 1, -1, -1):
        for c in range(len(owed)):
            up, down = send(going[c][0], right), send(going[c][1], left)
            if hop == reach - 1:
                ahead, behind = owed[c][hop], owed[c][-hop]
                up = jnp.concatenate([add(ahead[:half], up), ahead[half:]], axis=0)
                down = jnp.concatenate([behind[:half], add(behind[half:], down)], axis=0)
            elif hop:
                up, down = add(owed[c][hop], up), add(owed[c][-hop], down)
            going[c] = up, down
    moe = [o[0].astype(f32) + up.astype(f32) + down.astype(f32) for o, (up, down) in zip(owed, going)]
    return (tokens.astype(f32) + jnp.concatenate(moe, axis=1)[:, :width]).astype(bf16)


def solution(mesh):
    ep = mesh.shape["ep"]

    def shards(*arrays):
        whole_experts = arrays[-1].shape[0] == ep and ep == 16
        return (ring_shards if whole_experts else exchange_shards)(*arrays)

    return jax.shard_map(
        shards,
        mesh=mesh,
        in_specs=(
            P(("groups", "ep"), None),
            P(("groups", "ep"), None),
            P(("groups", "ep"), None),
            P(),
            P("ep", None, None),
            P("ep", None),
            P("ep", None, None),
            P(),
        ),
        out_specs=P(("groups", "ep"), None),
        check_vma=False,
    )
```

```python
import functools

import jax
import jax.numpy as jnp
from jax import lax
from jax.experimental import pallas as pl
from jax.experimental.pallas import tpu as pltpu
from jax.sharding import PartitionSpec as P

CAP = 18
LANES = 128
BLOCK = 768
NORM_MIB = 16
SMALL_MIB = 16
EXPERT_MIB = 50
COLUMNS = 1152
LEAD = -1
ACT_COLS = 256


def route_weights(gate_ints):
    int_gates = gate_ints.astype(jnp.float32)
    return int_gates / jnp.sum(int_gates, axis=1, keepdims=True)


def normalize(tokens, norm_gain):
    tok_float = tokens.astype(jnp.float32)
    row_scale = lax.rsqrt(jnp.mean(tok_float * tok_float, axis=1, keepdims=True) + 1e-05)
    return (tok_float * row_scale * norm_gain[None, :]).astype(jnp.bfloat16)


def exchange_shards(tokens, expert_ids, gate_ints, norm_gain, weight_in, bias_in, weight_out, bias_out):
    device_count = lax.axis_size("ep")
    expert_count = bias_out.shape[0]
    part_count = device_count // expert_count
    row_count, model_width = tokens.shape
    top_count = expert_ids.shape[1]
    capacity = CAP
    tok_float = tokens.astype(jnp.float32)
    normed = normalize(tokens, norm_gain)
    route_weight = route_weights(gate_ints)
    flat_ids = expert_ids.reshape(row_count * top_count)
    one_hot = (flat_ids[:, None] == jnp.arange(expert_count, dtype=jnp.int32)[None, :]).astype(jnp.int32)
    slot_rank = jnp.sum((jnp.cumsum(one_hot, axis=0) - one_hot) * one_hot, axis=1)
    slot_target = (flat_ids * capacity + slot_rank).reshape(row_count, top_count)
    slot_ids = jnp.arange(expert_count * capacity, dtype=jnp.int32)
    slot_match = slot_target[None, :, :] == slot_ids[:, None, None]
    picker = jnp.any(slot_match, axis=2).astype(jnp.bfloat16)
    placed = jnp.dot(picker, normed, preferred_element_type=jnp.float32).astype(jnp.bfloat16)
    combiner = jnp.transpose(jnp.sum(jnp.where(slot_match, route_weight[None, :, :], 0.0), axis=2))
    outgoing = jnp.broadcast_to(
        placed.reshape(expert_count, 1, capacity, model_width),
        (expert_count, part_count, capacity, model_width),
    ).reshape(device_count, capacity, model_width)
    arrived = lax.all_to_all(outgoing, "ep", split_axis=0, concat_axis=0, tiled=True)
    source_count, slot_count = arrived.shape[:2]
    flat_rows = arrived.reshape(source_count * slot_count, model_width)
    pre_act = jnp.dot(flat_rows, weight_in[0], preferred_element_type=jnp.float32) + bias_in[0][None, :]
    half_width = pre_act.shape[1] // 2
    gate_part = pre_act[:, :half_width]
    up_part = pre_act[:, half_width:]
    activated = (gate_part * jax.nn.sigmoid(1.702 * gate_part) * (up_part + 1.0)).astype(jnp.bfloat16)
    result = jnp.dot(activated, weight_out[0], preferred_element_type=jnp.float32).astype(jnp.bfloat16)
    returned = lax.all_to_all(
        result.reshape(source_count, slot_count, model_width), "ep", split_axis=0, concat_axis=0, tiled=True
    )
    part_sum = jnp.sum(
        returned.reshape(expert_count, part_count, capacity, model_width), axis=1, dtype=jnp.float32
    ).reshape(expert_count * capacity, model_width)
    moe_rows = jnp.dot(combiner, part_sum, precision=lax.Precision.HIGHEST)
    expert_hot = expert_ids[:, :, None] == jnp.arange(expert_count, dtype=jnp.int32)[None, None, :]
    expert_weight = jnp.sum(jnp.where(expert_hot, route_weight[:, :, None], 0.0), axis=1)
    bias_term = jnp.dot(expert_weight, bias_out, precision=lax.Precision.HIGHEST)
    return (tok_float + moe_rows + bias_term).astype(jnp.bfloat16)


def norm_kernel(top, tokens_ref, ids_ref, gates_ref, gain_ref, first_ref, second_ref):
    f32, bf16 = jnp.float32, jnp.bfloat16
    tok = tokens_ref[...].astype(f32)
    scale = lax.rsqrt(jnp.mean(tok * tok, axis=1, keepdims=True) + 1e-05)
    normed = (tok * scale * gain_ref[...][None, :]).astype(bf16)
    cut = tok.shape[1] - second_ref.shape[1]
    spare = first_ref.shape[1] - cut
    sub = lax.broadcasted_iota(jnp.int32, (top, spare), 0)
    lane = lax.broadcasted_iota(jnp.int32, (top, spare), 1)
    turn = (((0,), (0,)), ((), ()))
    tail = lax.dot_general(
        ids_ref[...].astype(f32), jnp.where(lane == sub, 1.0, 0.0), turn, preferred_element_type=f32
    ) + lax.dot_general(
        gates_ref[...].astype(f32), jnp.where(lane == sub + top, 1.0, 0.0), turn, preferred_element_type=f32
    )
    first_ref[:, :cut] = normed[:, :cut]
    first_ref[:, cut:] = tail.astype(bf16)
    second_ref[...] = normed[:, cut:]


def gather_rows(pieces, held):
    at = 0
    for ref in pieces:
        held[at : at + ref.shape[0]] = ref[...]
        at += ref.shape[0]


def route_kernel(top, cut, count, experts_ref, *refs):
    f32, bf16 = jnp.float32, jnp.bfloat16
    own_out, mate_out, picker_out, placer_out, held = refs[count:]
    gather_rows(refs[:count], held)
    tail = held[:, cut:]
    slots = own_out.shape[0]
    rows = tail.shape[0]
    sub = lax.broadcasted_iota(jnp.int32, (16, tail.shape[1]), 0)
    lane = lax.broadcasted_iota(jnp.int32, (16, tail.shape[1]), 1)
    pick_id = jnp.where((sub == lane) & (sub < top), 1.0, 0.0).astype(bf16)
    ids = lax.dot_general(pick_id, tail, (((1,), (1,)), ((), ())), preferred_element_type=f32)
    entry = lax.broadcasted_iota(jnp.int32, ids.shape, 0)
    first = lax.broadcasted_iota(jnp.int32, (rows, rows), 0)
    second = lax.broadcasted_iota(jnp.int32, (rows, rows), 1)
    upper = jnp.where(first <= second, 1.0, 0.0).astype(bf16)
    lower = jnp.where(first >= second, 1.0, 0.0).astype(bf16)
    tail_float = tail.astype(f32)
    tail_lane = lax.broadcasted_iota(jnp.int32, tail.shape, 1)
    slot = lax.broadcasted_iota(jnp.int32, (slots, rows), 0).astype(f32) + 1.0
    slot_lane = lax.broadcasted_iota(jnp.int32, (rows, slots), 1).astype(f32) + 1.0
    placers = []
    for i, out in enumerate((own_out, mate_out)):
        expert = experts_ref[0, i].astype(f32)
        named = jnp.sum(jnp.where((ids == expert) & (entry < top), 1.0, 0.0), axis=0, keepdims=True)
        number = jnp.dot(jnp.broadcast_to(named, (16, rows)).astype(bf16), upper, preferred_element_type=f32)[:1]
        picker = jnp.where((number == slot) & (named > 0.5), 1.0, 0.0).astype(bf16)
        picker_out[i * slots : (i + 1) * slots] = picker
        out[...] = jnp.dot(picker, held[...], preferred_element_type=f32).astype(bf16)
        named = jnp.sum(jnp.where((tail_float == expert) & (tail_lane < top), 1.0, 0.0), axis=1, keepdims=True)
        number = jnp.dot(lower, jnp.broadcast_to(named, (rows, LANES)).astype(bf16), preferred_element_type=f32)
        placers.append(jnp.where((number[:, :1] == slot_lane) & (named > 0.5), 1.0, 0.0))
    placer_out[...] = jnp.concatenate(placers, axis=1).astype(bf16)


def pick_kernel(count, picker_ref, *refs):
    own_out, mate_out, held = refs[count:]
    gather_rows(refs[:count], held)
    rows = jnp.dot(picker_ref[...], held[...], preferred_element_type=jnp.float32).astype(jnp.bfloat16)
    slots = own_out.shape[0]
    own_out[...] = rows[:slots]
    mate_out[...] = rows[slots:]


def slot_weights(tail, top, expert):
    f32 = jnp.float32
    lane = lax.broadcasted_iota(jnp.int32, tail.shape, 1)
    spare = tail.shape[1]
    first = lax.broadcasted_iota(jnp.int32, (spare, spare), 0)
    second = lax.broadcasted_iota(jnp.int32, (spare, spare), 1)
    shift = jnp.where((first == second + top) & (second < top), 1.0, 0.0).astype(jnp.bfloat16)
    gates = jnp.dot(tail, shift, preferred_element_type=f32)
    hit = (tail.astype(f32) == expert) & (lane < top)
    total = jnp.sum(gates, axis=1, keepdims=True)
    return jnp.sum(jnp.where(hit, gates, 0.0), axis=1, keepdims=True) / jnp.maximum(total, 1.0)


def activate(pre, act, start, end):
    hidden = act.shape[1]
    for at in range(start, end, ACT_COLS):
        to = min(at + ACT_COLS, end)
        gate = pre[:, at:to]
        up = pre[:, hidden + at : hidden + to]
        act[:, at:to] = (gate * jax.nn.sigmoid(1.702 * gate) * (up + 1.0)).astype(act.dtype)


def expert_kernel(
    top, steps_in, spans, experts_ref, own_first, mate_first, own_second, mate_second, win_ref, bin_ref, wout_hbm,
    bout_ref, own_a, mate_a, own_b, mate_b, rows_first, rows_second, pre, act, slot_weight, sems, *held,
):
    step = pl.program_id(0)
    f32, bf16 = jnp.float32, jnp.bfloat16
    slots, hidden, block = own_first.shape[0], act.shape[1], win_ref.shape[2]
    width = win_ref.shape[1]
    cut = width - own_second.shape[1]
    early = max((steps_in - 1) * block - hidden, 0) // LANES * LANES
    copies = [
        pltpu.make_async_copy(wout_hbm.at[0, :, pl.ds(at, size)], ref, sems.at[i])
        for i, ((at, size), ref) in enumerate(zip(spans, held))
    ]

    @pl.when(step == 0)
    def _():
        expert = experts_ref[0, 0].astype(f32)
        for i, (low, high) in enumerate(((own_first, own_second), (mate_first, mate_second))):
            rows_first[i * slots : (i + 1) * slots] = low[...]
            rows_second[i * slots : (i + 1) * slots] = high[...]
            weight = slot_weights(low[:, cut:], top, expert)
            slot_weight[i * slots : (i + 1) * slots] = jnp.broadcast_to(weight, (slots, LANES))

    for i, copy in enumerate(copies):

        @pl.when(step == max(steps_in - len(copies) + i - LEAD, 0))
        def _():
            copy.start()

    def first_layer(at):
        total = jnp.dot(rows_first[:, :cut], win_ref[0, :cut], preferred_element_type=f32)
        total += jnp.dot(rows_second[...], win_ref[0, cut:], preferred_element_type=f32)
        pre[:, pl.ds(at, block)] = total + bin_ref[...]

    @pl.when(step < steps_in - 1)
    def _():
        first_layer(pl.multiple_of(step * block, block))

    @pl.when(step == steps_in - 1)
    def _():
        first_layer((steps_in - 1) * block)
        activate(pre, act, 0, early)

    @pl.when(step == steps_in)
    def _():
        activate(pre, act, early, hidden)
        edge = own_a.shape[1]
        for copy, ref, (at, size) in zip(copies, held, spans):
            copy.wait()
            result = jnp.dot(act[:, :early], ref[:early], preferred_element_type=f32)
            result += jnp.dot(act[:, early:], ref[early:], preferred_element_type=f32)
            result = ((result + bout_ref[:, at : at + size]) * slot_weight[:, :1]).astype(bf16)
            inside = min(max(edge - at, 0), size)
            for row, low, high in ((0, own_a, own_b), (slots, mate_a, mate_b)):
                if inside:
                    low[:, at : at + inside] = result[row : row + slots, :inside]
                if inside < size:
                    high[:, at + inside - edge : at + size - edge] = result[row : row + slots, inside:]
        for ref in (own_b, mate_b):
            ref[:, width - edge :] = jnp.zeros((slots, ref.shape[1] - (width - edge)), bf16)


def spread_kernel(placer_ref, own_ref, mate_ref, *out_refs):
    slots = own_ref.shape[0]
    f32 = jnp.float32
    total = jnp.dot(placer_ref[:, :slots], own_ref[...], preferred_element_type=f32)
    total += jnp.dot(placer_ref[:, slots:], mate_ref[...], preferred_element_type=f32)
    at = 0
    for ref in out_refs:
        ref[...] = total[at : at + ref.shape[0]].astype(ref.dtype)
        at += ref.shape[0]


def params(mib):
    return pltpu.CompilerParams(vmem_limit_bytes=mib * 2**20)


def cost(macs, moved):
    return pl.CostEstimate(flops=2 * macs, bytes_accessed=moved, transcendentals=0)


def ring_shards(tokens, expert_ids, gate_ints, norm_gain, weight_in, bias_in, weight_out, bias_out):
    device_count = lax.axis_size("ep")
    chips = device_count // 2
    reach = chips // 2
    ring = list(range(0, chips, 2)) + list(range(chips - 1, 0, -2))
    right = [(ring[i] * 2 + k, ring[(i + 1) % chips] * 2 + k) for i in range(chips) for k in range(2)]
    left = [(b, a) for a, b in right]
    mate = [(i, i ^ 1) for i in range(device_count)]
    send = lambda value, pairs: lax.ppermute(value, "ep", pairs)
    bf16, f32 = jnp.bfloat16, jnp.float32
    row_count, width = tokens.shape
    top = expert_ids.shape[1]
    hidden = weight_out.shape[1]
    half = row_count // 2
    lanes = [2 * BLOCK, width + -width % LANES - 2 * BLOCK]
    cut = width - lanes[1]
    slots, all_rows = chips * CAP, chips * row_count
    vmem = pl.BlockSpec(memory_space=pltpu.VMEM)
    smem = pl.BlockSpec(memory_space=pltpu.SMEM)
    shape = lambda rows, cols, dtype=bf16: jax.ShapeDtypeStruct((rows, cols), dtype)

    chains = pl.pallas_call(
        functools.partial(norm_kernel, top),
        in_specs=[vmem] * 4,
        out_specs=[vmem] * 2,
        out_shape=[shape(row_count, w) for w in lanes],
        compiler_params=params(NORM_MIB),
    )(tokens, expert_ids.T, gate_ints.T, norm_gain)
    me = lax.axis_index("ep").astype(jnp.int32)
    experts = jnp.stack([me, me ^ 1]).reshape(1, 2)
    bias_row = lax.dynamic_slice_in_dim(bias_out, me, 1, axis=0)

    held = [[chain] for chain in chains]
    going = [(chain, chain) for chain in chains]
    for hop in range(1, reach + 1):
        for c in range(len(chains)):
            to_right, to_left = going[c]
            if hop == reach:
                to_right, to_left = to_right[:half], to_left[half:]
                if c:
                    to_right, to_left, _ = lax.optimization_barrier((to_right, to_left, waited))
                waited = going[c]
            going[c] = send(to_right, right), send(to_left, left)
            held[c] += going[c]
    order = [0]
    for hop in range(1, reach):
        order += [-hop, hop]
    own_first, mate_first, picker, placer = pl.pallas_call(
        functools.partial(route_kernel, top, cut, len(held[0])),
        in_specs=[smem] + [vmem] * len(held[0]),
        out_specs=[vmem] * 4,
        out_shape=[shape(slots, lanes[0])] * 2 + [shape(2 * slots, all_rows), shape(all_rows, 2 * slots)],
        scratch_shapes=[pltpu.VMEM((all_rows, lanes[0]), bf16)],
        cost_estimate=cost(2 * slots * all_rows * lanes[0], 2**20),
        compiler_params=params(SMALL_MIB),
    )(experts, *held[0])
    mate_first = send(mate_first, mate)
    own_second, mate_second = pl.pallas_call(
        functools.partial(pick_kernel, len(held[1])),
        in_specs=[vmem] * (1 + len(held[1])),
        out_specs=[vmem] * 2,
        out_shape=[shape(slots, lanes[1])] * 2,
        scratch_shapes=[pltpu.VMEM((all_rows, lanes[1]), bf16)],
        cost_estimate=cost(2 * slots * all_rows * lanes[1], 2**20),
        compiler_params=params(SMALL_MIB),
    )(picker, *held[1])
    mate_second = send(mate_second, mate)

    steps_in = pl.cdiv(2 * hidden, COLUMNS)
    spans = [(at, min(COLUMNS, width - at)) for at in range(0, width, COLUMNS)]
    first = lambda j: jnp.minimum(j, steps_in - 1)
    whole = lambda rows, cols: pl.BlockSpec((rows, cols), lambda j: (0, 0), pipeline_mode=pl.Buffered(1))
    own_a, mate_a, own_b, mate_b = pl.pallas_call(
        functools.partial(expert_kernel, top, steps_in, spans),
        grid=(steps_in + 1,),
        in_specs=[
            smem, whole(slots, lanes[0]), whole(slots, lanes[0]), whole(slots, lanes[1]), whole(slots, lanes[1]),
            pl.BlockSpec((1, width, COLUMNS), lambda j: (0, 0, first(j))),
            pl.BlockSpec((1, COLUMNS), lambda j: (0, first(j))),
            pl.BlockSpec(memory_space=pl.ANY),
            whole(1, width),
        ],
        out_specs=[whole(slots, w) for w in (lanes[0], lanes[0], lanes[1], lanes[1])],
        out_shape=[shape(slots, w) for w in (lanes[0], lanes[0], lanes[1], lanes[1])],
        scratch_shapes=[
            pltpu.VMEM((2 * slots, lanes[0]), bf16),
            pltpu.VMEM((2 * slots, lanes[1]), bf16),
            pltpu.VMEM((2 * slots, steps_in * COLUMNS), f32),
            pltpu.VMEM((2 * slots, hidden), bf16),
            pltpu.VMEM((2 * slots, LANES), f32),
            pltpu.SemaphoreType.DMA((len(spans),)),
        ]
        + [pltpu.VMEM((hidden, size), bf16) for _, size in spans],
        cost_estimate=cost(2 * slots * width * 3 * hidden, 6 * width * hidden),
        compiler_params=params(EXPERT_MIB),
    )(experts, own_first, mate_first, own_second, mate_second, weight_in, bias_in, weight_out, bias_row)

    heights = [row_count] * (chips - 1) + [half, half]
    add = lambda a, b: (a.astype(f32) + b.astype(f32)).astype(bf16)

    def spread(own, other):
        sums = pl.pallas_call(
            spread_kernel,
            in_specs=[vmem] * 3,
            out_specs=[vmem] * len(heights),
            out_shape=[shape(rows, own.shape[1]) for rows in heights],
            cost_estimate=cost(2 * slots * all_rows * own.shape[1], 2**20),
            compiler_params=params(SMALL_MIB),
        )(placer, own, send(other, mate))
        return dict(zip(order + ["right", "left"], sums))

    owed = [spread(own_a, mate_a), spread(own_b, mate_b)]
    going = [(o["right"], o["left"]) for o in owed]
    for hop in range(reach - 1, -1, -1):
        for c in range(len(owed)):
            up, down = send(going[c][0], right), send(going[c][1], left)
            if hop == reach - 1:
                ahead, behind = owed[c][hop], owed[c][-hop]
                up = jnp.concatenate([add(ahead[:half], up), ahead[half:]], axis=0)
                down = jnp.concatenate([behind[:half], add(behind[half:], down)], axis=0)
            elif hop:
                up, down = add(owed[c][hop], up), add(owed[c][-hop], down)
            going[c] = up, down
    moe = [o[0].astype(f32) + up.astype(f32) + down.astype(f32) for o, (up, down) in zip(owed, going)]
    return (tokens.astype(f32) + jnp.concatenate(moe, axis=1)[:, :width]).astype(bf16)


def solution(mesh):
    ep = mesh.shape["ep"]

    def shards(*arrays):
        whole_experts = arrays[-1].shape[0] == ep and ep == 16
        return (ring_shards if whole_experts else exchange_shards)(*arrays)

    return jax.shard_map(
        shards,
        mesh=mesh,
        in_specs=(
            P(("groups", "ep"), None),
            P(("groups", "ep"), None),
            P(("groups", "ep"), None),
            P(),
            P("ep", None, None),
            P("ep", None),
            P("ep", None, None),
            P(),
        ),
        out_specs=P(("groups", "ep"), None),
        check_vma=False,
    )
```

```python
import functools

import jax
import jax.numpy as jnp
from jax import lax
from jax.experimental import pallas as pl
from jax.experimental.pallas import tpu as pltpu
from jax.sharding import PartitionSpec as P

CAP = 18
LANES = 128
BLOCK = 768
NORM_MIB = 16
SMALL_MIB = 16
PICK_MIB = 16
EXPERT_MIB = 50
COLUMNS = 1152
ACT_COLS = 256


def route_weights(gate_ints):
    int_gates = gate_ints.astype(jnp.float32)
    return int_gates / jnp.sum(int_gates, axis=1, keepdims=True)


def normalize(tokens, norm_gain):
    tok_float = tokens.astype(jnp.float32)
    row_scale = lax.rsqrt(jnp.mean(tok_float * tok_float, axis=1, keepdims=True) + 1e-05)
    return (tok_float * row_scale * norm_gain[None, :]).astype(jnp.bfloat16)


def exchange_shards(tokens, expert_ids, gate_ints, norm_gain, weight_in, bias_in, weight_out, bias_out):
    device_count = lax.axis_size("ep")
    expert_count = bias_out.shape[0]
    part_count = device_count // expert_count
    row_count, model_width = tokens.shape
    top_count = expert_ids.shape[1]
    capacity = CAP
    tok_float = tokens.astype(jnp.float32)
    normed = normalize(tokens, norm_gain)
    route_weight = route_weights(gate_ints)
    flat_ids = expert_ids.reshape(row_count * top_count)
    one_hot = (flat_ids[:, None] == jnp.arange(expert_count, dtype=jnp.int32)[None, :]).astype(jnp.int32)
    slot_rank = jnp.sum((jnp.cumsum(one_hot, axis=0) - one_hot) * one_hot, axis=1)
    slot_target = (flat_ids * capacity + slot_rank).reshape(row_count, top_count)
    slot_ids = jnp.arange(expert_count * capacity, dtype=jnp.int32)
    slot_match = slot_target[None, :, :] == slot_ids[:, None, None]
    picker = jnp.any(slot_match, axis=2).astype(jnp.bfloat16)
    placed = jnp.dot(picker, normed, preferred_element_type=jnp.float32).astype(jnp.bfloat16)
    combiner = jnp.transpose(jnp.sum(jnp.where(slot_match, route_weight[None, :, :], 0.0), axis=2))
    outgoing = jnp.broadcast_to(
        placed.reshape(expert_count, 1, capacity, model_width),
        (expert_count, part_count, capacity, model_width),
    ).reshape(device_count, capacity, model_width)
    arrived = lax.all_to_all(outgoing, "ep", split_axis=0, concat_axis=0, tiled=True)
    source_count, slot_count = arrived.shape[:2]
    flat_rows = arrived.reshape(source_count * slot_count, model_width)
    pre_act = jnp.dot(flat_rows, weight_in[0], preferred_element_type=jnp.float32) + bias_in[0][None, :]
    half_width = pre_act.shape[1] // 2
    gate_part = pre_act[:, :half_width]
    up_part = pre_act[:, half_width:]
    activated = (gate_part * jax.nn.sigmoid(1.702 * gate_part) * (up_part + 1.0)).astype(jnp.bfloat16)
    result = jnp.dot(activated, weight_out[0], preferred_element_type=jnp.float32).astype(jnp.bfloat16)
    returned = lax.all_to_all(
        result.reshape(source_count, slot_count, model_width), "ep", split_axis=0, concat_axis=0, tiled=True
    )
    part_sum = jnp.sum(
        returned.reshape(expert_count, part_count, capacity, model_width), axis=1, dtype=jnp.float32
    ).reshape(expert_count * capacity, model_width)
    moe_rows = jnp.dot(combiner, part_sum, precision=lax.Precision.HIGHEST)
    expert_hot = expert_ids[:, :, None] == jnp.arange(expert_count, dtype=jnp.int32)[None, None, :]
    expert_weight = jnp.sum(jnp.where(expert_hot, route_weight[:, :, None], 0.0), axis=1)
    bias_term = jnp.dot(expert_weight, bias_out, precision=lax.Precision.HIGHEST)
    return (tok_float + moe_rows + bias_term).astype(jnp.bfloat16)


def norm_kernel(top, tokens_ref, ids_ref, gates_ref, gain_ref, first_ref, second_ref):
    f32, bf16 = jnp.float32, jnp.bfloat16
    tok = tokens_ref[...].astype(f32)
    scale = lax.rsqrt(jnp.mean(tok * tok, axis=1, keepdims=True) + 1e-05)
    normed = (tok * scale * gain_ref[...][None, :]).astype(bf16)
    cut = tok.shape[1] - second_ref.shape[1]
    spare = first_ref.shape[1] - cut
    sub = lax.broadcasted_iota(jnp.int32, (top, spare), 0)
    lane = lax.broadcasted_iota(jnp.int32, (top, spare), 1)
    turn = (((0,), (0,)), ((), ()))
    tail = lax.dot_general(
        ids_ref[...].astype(f32), jnp.where(lane == sub, 1.0, 0.0), turn, preferred_element_type=f32
    ) + lax.dot_general(
        gates_ref[...].astype(f32), jnp.where(lane == sub + top, 1.0, 0.0), turn, preferred_element_type=f32
    )
    first_ref[:, :cut] = normed[:, :cut]
    first_ref[:, cut:] = tail.astype(bf16)
    second_ref[...] = normed[:, cut:]


def gather_rows(pieces, held):
    at = 0
    for ref in pieces:
        held[at : at + ref.shape[0]] = ref[...]
        at += ref.shape[0]


def route_kernel(top, cut, count, experts_ref, *refs):
    f32, bf16 = jnp.float32, jnp.bfloat16
    own_out, mate_out, picker_out, placer_out, held = refs[count:]
    gather_rows(refs[:count], held)
    tail = held[:, cut:]
    slots = own_out.shape[0]
    rows = tail.shape[0]
    sub = lax.broadcasted_iota(jnp.int32, (16, tail.shape[1]), 0)
    lane = lax.broadcasted_iota(jnp.int32, (16, tail.shape[1]), 1)
    pick_id = jnp.where((sub == lane) & (sub < top), 1.0, 0.0).astype(bf16)
    ids = lax.dot_general(pick_id, tail, (((1,), (1,)), ((), ())), preferred_element_type=f32)
    entry = lax.broadcasted_iota(jnp.int32, ids.shape, 0)
    first = lax.broadcasted_iota(jnp.int32, (rows, rows), 0)
    second = lax.broadcasted_iota(jnp.int32, (rows, rows), 1)
    upper = jnp.where(first <= second, 1.0, 0.0).astype(bf16)
    lower = jnp.where(first >= second, 1.0, 0.0).astype(bf16)
    tail_float = tail.astype(f32)
    tail_lane = lax.broadcasted_iota(jnp.int32, tail.shape, 1)
    slot = lax.broadcasted_iota(jnp.int32, (slots, rows), 0).astype(f32) + 1.0
    slot_lane = lax.broadcasted_iota(jnp.int32, (rows, slots), 1).astype(f32) + 1.0
    placers = []
    for i, out in enumerate((own_out, mate_out)):
        expert = experts_ref[0, i].astype(f32)
        named = jnp.sum(jnp.where((ids == expert) & (entry < top), 1.0, 0.0), axis=0, keepdims=True)
        number = jnp.dot(jnp.broadcast_to(named, (16, rows)).astype(bf16), upper, preferred_element_type=f32)[:1]
        picker = jnp.where((number == slot) & (named > 0.5), 1.0, 0.0).astype(bf16)
        picker_out[i * slots : (i + 1) * slots] = picker
        out[...] = jnp.dot(picker, held[...], preferred_element_type=f32).astype(bf16)
        named = jnp.sum(jnp.where((tail_float == expert) & (tail_lane < top), 1.0, 0.0), axis=1, keepdims=True)
        number = jnp.dot(lower, jnp.broadcast_to(named, (rows, LANES)).astype(bf16), preferred_element_type=f32)
        placers.append(jnp.where((number[:, :1] == slot_lane) & (named > 0.5), 1.0, 0.0))
    placer_out[...] = jnp.concatenate(placers, axis=1).astype(bf16)


def pick_kernel(count, picker_ref, first_ref, *refs):
    own_out, mate_out, held = refs[count:]
    gather_rows(refs[:count], held)
    rows = jnp.dot(picker_ref[...], held[...], preferred_element_type=jnp.float32).astype(jnp.bfloat16)
    slots, edge = first_ref.shape
    own_out[:, :edge] = first_ref[...]
    own_out[:, edge:] = rows[:slots]
    mate_out[...] = rows[slots:]


def slot_weights(tail, top, expert):
    f32 = jnp.float32
    lane = lax.broadcasted_iota(jnp.int32, tail.shape, 1)
    spare = tail.shape[1]
    first = lax.broadcasted_iota(jnp.int32, (spare, spare), 0)
    second = lax.broadcasted_iota(jnp.int32, (spare, spare), 1)
    shift = jnp.where((first == second + top) & (second < top), 1.0, 0.0).astype(jnp.bfloat16)
    gates = jnp.dot(tail, shift, preferred_element_type=f32)
    hit = (tail.astype(f32) == expert) & (lane < top)
    total = jnp.sum(gates, axis=1, keepdims=True)
    return jnp.sum(jnp.where(hit, gates, 0.0), axis=1, keepdims=True) / jnp.maximum(total, 1.0)


def activate(pre, act, start, end):
    hidden = act.shape[1]
    for at in range(start, end, ACT_COLS):
        to = min(at + ACT_COLS, end)
        gate = pre[:, at:to]
        up = pre[:, hidden + at : hidden + to]
        act[:, at:to] = (gate * jax.nn.sigmoid(1.702 * gate) * (up + 1.0)).astype(act.dtype)


def expert_kernel(
    top, steps_in, spans, experts_ref, own_rows, mate_first, mate_second, win_ref, bias_ref, wout_hbm,
    own_a, mate_a, own_b, mate_b, rows_first, rows_second, pre, act, slot_weight, sems, *held,
):
    step = pl.program_id(0)
    f32, bf16 = jnp.float32, jnp.bfloat16
    slots, hidden, block = mate_first.shape[0], act.shape[1], win_ref.shape[2]
    width = win_ref.shape[1]
    edge = mate_first.shape[1]
    cut = width - mate_second.shape[1]
    early = max((steps_in - 1) * block - hidden, 0) // LANES * LANES
    copies = [
        pltpu.make_async_copy(wout_hbm.at[0, :, pl.ds(at, size)], ref, sems.at[i])
        for i, ((at, size), ref) in enumerate(zip(spans, held))
    ]

    @pl.when(step == 0)
    def _():
        expert = experts_ref[0, 0].astype(f32)
        rows_first[:slots] = own_rows[:, :edge]
        rows_first[slots:] = mate_first[...]
        rows_second[:slots] = own_rows[:, edge:]
        rows_second[slots:] = mate_second[...]
        for i in range(2):
            weight = slot_weights(rows_first[i * slots : (i + 1) * slots, cut:], top, expert)
            slot_weight[i * slots : (i + 1) * slots] = jnp.broadcast_to(weight, (slots, LANES))

    for i, copy in enumerate(copies):

        @pl.when(step == steps_in - (1 if i == 0 else 0))
        def _():
            copy.start()

    def first_layer(at):
        total = jnp.dot(rows_first[:, :cut], win_ref[0, :cut], preferred_element_type=f32)
        total += jnp.dot(rows_second[...], win_ref[0, cut:], preferred_element_type=f32)
        pre[:, pl.ds(at, block)] = total + bias_ref[:, pl.ds(at, block)]

    @pl.when(step < steps_in - 1)
    def _():
        first_layer(pl.multiple_of(step * block, block))

    @pl.when(step == steps_in - 1)
    def _():
        first_layer((steps_in - 1) * block)
        activate(pre, act, 0, early)

    @pl.when(step == steps_in)
    def _():
        activate(pre, act, early, hidden)
        edge = own_a.shape[1]
        for copy, ref, (at, size) in zip(copies, held, spans):
            if at == 0:
                copy.wait()
            elif at == spans[1][0]:
                for later in copies[1:]:
                    later.wait()
            result = jnp.dot(act[:, :early], ref[:early], preferred_element_type=f32)
            result += jnp.dot(act[:, early:], ref[early:], preferred_element_type=f32)
            result = ((result + bias_ref[:, 2 * hidden + at : 2 * hidden + at + size]) * slot_weight[:, :1]).astype(bf16)
            inside = min(max(edge - at, 0), size)
            for row, low, high in ((0, own_a, own_b), (slots, mate_a, mate_b)):
                if inside:
                    low[:, at : at + inside] = result[row : row + slots, :inside]
                if inside < size:
                    high[:, at + inside - edge : at + size - edge] = result[row : row + slots, inside:]
        for ref in (own_b, mate_b):
            ref[:, width - edge :] = jnp.zeros((slots, ref.shape[1] - (width - edge)), bf16)


def spread_kernel(placer_ref, own_ref, mate_ref, *out_refs):
    slots = own_ref.shape[0]
    f32 = jnp.float32
    total = jnp.dot(placer_ref[:, :slots], own_ref[...], preferred_element_type=f32)
    total += jnp.dot(placer_ref[:, slots:], mate_ref[...], preferred_element_type=f32)
    at = 0
    for ref in out_refs:
        ref[...] = total[at : at + ref.shape[0]].astype(ref.dtype)
        at += ref.shape[0]


def params(mib):
    return pltpu.CompilerParams(vmem_limit_bytes=mib * 2**20)


def cost(macs, moved):
    return pl.CostEstimate(flops=2 * macs, bytes_accessed=moved, transcendentals=0)


def ring_shards(tokens, expert_ids, gate_ints, norm_gain, weight_in, bias_in, weight_out, bias_out):
    device_count = lax.axis_size("ep")
    chips = device_count // 2
    reach = chips // 2
    ring = list(range(0, chips, 2)) + list(range(chips - 1, 0, -2))
    right = [(ring[i] * 2 + k, ring[(i + 1) % chips] * 2 + k) for i in range(chips) for k in range(2)]
    left = [(b, a) for a, b in right]
    mate = [(i, i ^ 1) for i in range(device_count)]
    send = lambda value, pairs: lax.ppermute(value, "ep", pairs)
    bf16, f32 = jnp.bfloat16, jnp.float32
    row_count, width = tokens.shape
    top = expert_ids.shape[1]
    hidden = weight_out.shape[1]
    lanes = [2 * BLOCK, width + -width % LANES - 2 * BLOCK]
    cut = width - lanes[1]
    slots, all_rows = chips * CAP, chips * row_count
    vmem = pl.BlockSpec(memory_space=pltpu.VMEM)
    smem = pl.BlockSpec(memory_space=pltpu.SMEM)
    shape = lambda rows, cols, dtype=bf16: jax.ShapeDtypeStruct((rows, cols), dtype)

    chains = pl.pallas_call(
        functools.partial(norm_kernel, top),
        in_specs=[vmem] * 4,
        out_specs=[vmem] * 2,
        out_shape=[shape(row_count, w) for w in lanes],
        compiler_params=params(NORM_MIB),
    )(tokens, expert_ids.T, gate_ints.T, norm_gain)
    me = lax.axis_index("ep").astype(jnp.int32)
    experts = jnp.stack([me, me ^ 1]).reshape(1, 2)
    biases = jnp.concatenate([bias_in, lax.dynamic_slice_in_dim(bias_out, me, 1, axis=0)], axis=1)

    held = [[chain] for chain in chains]
    going = [[chain, chain] for chain in chains]
    for hop in range(1, reach + 1):
        for c in range(len(chains)):
            for way, pairs in enumerate((right, left)):
                if hop < reach or way == c:
                    going[c][way] = send(going[c][way], pairs)
                    held[c].append(going[c][way])
    order = [0]
    for hop in range(1, reach):
        order += [-hop, hop]
    order.append(reach)
    own_first, mate_first, picker, placer = pl.pallas_call(
        functools.partial(route_kernel, top, cut, len(held[0])),
        in_specs=[smem] + [vmem] * len(held[0]),
        out_specs=[vmem] * 4,
        out_shape=[shape(slots, lanes[0])] * 2 + [shape(2 * slots, all_rows), shape(all_rows, 2 * slots)],
        scratch_shapes=[pltpu.VMEM((all_rows, lanes[0]), bf16)],
        cost_estimate=cost(2 * slots * all_rows * lanes[0], 2**20),
        compiler_params=params(PICK_MIB),
    )(experts, *held[0])
    mate_first = send(mate_first, mate)
    own_rows, mate_second = pl.pallas_call(
        functools.partial(pick_kernel, len(held[1])),
        in_specs=[vmem] * (2 + len(held[1])),
        out_specs=[vmem] * 2,
        out_shape=[shape(slots, sum(lanes)), shape(slots, lanes[1])],
        scratch_shapes=[pltpu.VMEM((all_rows, lanes[1]), bf16)],
        cost_estimate=cost(2 * slots * all_rows * lanes[1], 2**20),
        compiler_params=params(PICK_MIB),
    )(picker, own_first, *held[1])
    mate_second = send(mate_second, mate)

    steps_in = pl.cdiv(2 * hidden, COLUMNS)
    spans = [(at, min(COLUMNS, width - at)) for at in range(0, width, COLUMNS)]
    first = lambda j: jnp.minimum(j, steps_in - 1)
    whole = lambda rows, cols: pl.BlockSpec((rows, cols), lambda j: (0, 0), pipeline_mode=pl.Buffered(1))
    own_a, mate_a, own_b, mate_b = pl.pallas_call(
        functools.partial(expert_kernel, top, steps_in, spans),
        grid=(steps_in + 1,),
        in_specs=[
            smem, whole(slots, sum(lanes)), whole(slots, lanes[0]), whole(slots, lanes[1]),
            pl.BlockSpec((1, width, COLUMNS), lambda j: (0, 0, first(j))),
            whole(1, 2 * hidden + width),
            pl.BlockSpec(memory_space=pl.ANY),
        ],
        out_specs=[whole(slots, w) for w in (lanes[0], lanes[0], lanes[1], lanes[1])],
        out_shape=[shape(slots, w) for w in (lanes[0], lanes[0], lanes[1], lanes[1])],
        scratch_shapes=[
            pltpu.VMEM((2 * slots, lanes[0]), bf16),
            pltpu.VMEM((2 * slots, lanes[1]), bf16),
            pltpu.VMEM((2 * slots, steps_in * COLUMNS), f32),
            pltpu.VMEM((2 * slots, hidden), bf16),
            pltpu.VMEM((2 * slots, LANES), f32),
            pltpu.SemaphoreType.DMA((len(spans),)),
        ]
        + [pltpu.VMEM((hidden, size), bf16) for _, size in spans],
        cost_estimate=cost(2 * slots * width * 3 * hidden, 6 * width * hidden),
        compiler_params=params(EXPERT_MIB),
    )(experts, own_rows, mate_first, mate_second, weight_in, biases, weight_out)

    add = lambda a, b: (a.astype(f32) + b.astype(f32)).astype(bf16)
    owed = []
    for own, other in ((own_a, mate_a), (own_b, mate_b)):
        sums = pl.pallas_call(
            spread_kernel,
            in_specs=[vmem] * 3,
            out_specs=[vmem] * chips,
            out_shape=[shape(row_count, own.shape[1])] * chips,
            cost_estimate=cost(2 * slots * all_rows * own.shape[1], 2**20),
            compiler_params=params(SMALL_MIB),
        )(placer, own, send(other, mate))
        owed.append(dict(zip(order, sums)))
    going = [[None, None] for _ in owed]
    for hop in range(reach, 0, -1):
        for c in range(len(owed)):
            for way, pairs in enumerate((right, left)):
                if hop < reach or way == c:
                    mine = owed[c][hop if way == 0 or hop == reach else -hop]
                    passed = mine if going[c][way] is None else add(mine, going[c][way])
                    going[c][way] = send(passed, pairs)
    moe = [o[0].astype(f32) + up.astype(f32) + down.astype(f32) for o, (up, down) in zip(owed, going)]
    return (tokens.astype(f32) + jnp.concatenate(moe, axis=1)[:, :width]).astype(bf16)


def solution(mesh):
    ep = mesh.shape["ep"]

    def shards(*arrays):
        whole_experts = arrays[-1].shape[0] == ep and ep == 16
        return (ring_shards if whole_experts else exchange_shards)(*arrays)

    return jax.shard_map(
        shards,
        mesh=mesh,
        in_specs=(
            P(("groups", "ep"), None),
            P(("groups", "ep"), None),
            P(("groups", "ep"), None),
            P(),
            P("ep", None, None),
            P("ep", None),
            P("ep", None, None),
            P(),
        ),
        out_specs=P(("groups", "ep"), None),
        check_vma=False,
    )
```

```python
import functools

import jax
import jax.numpy as jnp
from jax import lax
from jax.experimental import pallas as pl
from jax.experimental.pallas import tpu as pltpu
from jax.sharding import PartitionSpec as P

CAP = 18
LANES = 128
BLOCK = 768
NORM_MIB = 16
SMALL_MIB = 16
PICK_MIB = 16
EXPERT_MIB = 50
COLUMNS = 1152
ACT_COLS = 256


def route_weights(gate_ints):
    int_gates = gate_ints.astype(jnp.float32)
    return int_gates / jnp.sum(int_gates, axis=1, keepdims=True)


def normalize(tokens, norm_gain):
    tok_float = tokens.astype(jnp.float32)
    row_scale = lax.rsqrt(jnp.mean(tok_float * tok_float, axis=1, keepdims=True) + 1e-05)
    return (tok_float * row_scale * norm_gain[None, :]).astype(jnp.bfloat16)


def exchange_shards(tokens, expert_ids, gate_ints, norm_gain, weight_in, bias_in, weight_out, bias_out):
    device_count = lax.axis_size("ep")
    expert_count = bias_out.shape[0]
    part_count = device_count // expert_count
    row_count, model_width = tokens.shape
    top_count = expert_ids.shape[1]
    capacity = CAP
    tok_float = tokens.astype(jnp.float32)
    normed = normalize(tokens, norm_gain)
    route_weight = route_weights(gate_ints)
    flat_ids = expert_ids.reshape(row_count * top_count)
    one_hot = (flat_ids[:, None] == jnp.arange(expert_count, dtype=jnp.int32)[None, :]).astype(jnp.int32)
    slot_rank = jnp.sum((jnp.cumsum(one_hot, axis=0) - one_hot) * one_hot, axis=1)
    slot_target = (flat_ids * capacity + slot_rank).reshape(row_count, top_count)
    slot_ids = jnp.arange(expert_count * capacity, dtype=jnp.int32)
    slot_match = slot_target[None, :, :] == slot_ids[:, None, None]
    picker = jnp.any(slot_match, axis=2).astype(jnp.bfloat16)
    placed = jnp.dot(picker, normed, preferred_element_type=jnp.float32).astype(jnp.bfloat16)
    combiner = jnp.transpose(jnp.sum(jnp.where(slot_match, route_weight[None, :, :], 0.0), axis=2))
    outgoing = jnp.broadcast_to(
        placed.reshape(expert_count, 1, capacity, model_width),
        (expert_count, part_count, capacity, model_width),
    ).reshape(device_count, capacity, model_width)
    arrived = lax.all_to_all(outgoing, "ep", split_axis=0, concat_axis=0, tiled=True)
    source_count, slot_count = arrived.shape[:2]
    flat_rows = arrived.reshape(source_count * slot_count, model_width)
    pre_act = jnp.dot(flat_rows, weight_in[0], preferred_element_type=jnp.float32) + bias_in[0][None, :]
    half_width = pre_act.shape[1] // 2
    gate_part = pre_act[:, :half_width]
    up_part = pre_act[:, half_width:]
    activated = (gate_part * jax.nn.sigmoid(1.702 * gate_part) * (up_part + 1.0)).astype(jnp.bfloat16)
    result = jnp.dot(activated, weight_out[0], preferred_element_type=jnp.float32).astype(jnp.bfloat16)
    returned = lax.all_to_all(
        result.reshape(source_count, slot_count, model_width), "ep", split_axis=0, concat_axis=0, tiled=True
    )
    part_sum = jnp.sum(
        returned.reshape(expert_count, part_count, capacity, model_width), axis=1, dtype=jnp.float32
    ).reshape(expert_count * capacity, model_width)
    moe_rows = jnp.dot(combiner, part_sum, precision=lax.Precision.HIGHEST)
    expert_hot = expert_ids[:, :, None] == jnp.arange(expert_count, dtype=jnp.int32)[None, None, :]
    expert_weight = jnp.sum(jnp.where(expert_hot, route_weight[:, :, None], 0.0), axis=1)
    bias_term = jnp.dot(expert_weight, bias_out, precision=lax.Precision.HIGHEST)
    return (tok_float + moe_rows + bias_term).astype(jnp.bfloat16)


def norm_kernel(tokens_ref, named_ref, gain_ref, first_ref, second_ref):
    f32, bf16 = jnp.float32, jnp.bfloat16
    tok = tokens_ref[...].astype(f32)
    scale = lax.rsqrt(jnp.mean(tok * tok, axis=1, keepdims=True) + 1e-05)
    normed = (tok * scale * gain_ref[...][None, :]).astype(bf16)
    cut = tok.shape[1] - second_ref.shape[1]
    spare = first_ref.shape[1] - cut
    entries = named_ref.shape[0]
    sub = lax.broadcasted_iota(jnp.int32, (entries, spare), 0)
    lane = lax.broadcasted_iota(jnp.int32, (entries, spare), 1)
    tail = lax.dot_general(
        named_ref[...].astype(f32),
        jnp.where(lane == sub, 1.0, 0.0),
        (((0,), (0,)), ((), ())),
        preferred_element_type=f32,
    )
    first_ref[:, :cut] = normed[:, :cut]
    first_ref[:, cut:] = tail.astype(bf16)
    second_ref[...] = normed[:, cut:]


def gather_rows(pieces, held):
    at = 0
    for ref in pieces:
        held[at : at + ref.shape[0]] = ref[...]
        at += ref.shape[0]


def route_kernel(top, cut, count, experts_ref, *refs):
    f32, bf16 = jnp.float32, jnp.bfloat16
    own_out, mate_out, picker_out, placer_out, held = refs[count:]
    gather_rows(refs[:count], held)
    tail = held[:, cut:]
    slots = own_out.shape[0]
    rows = tail.shape[0]
    sub = lax.broadcasted_iota(jnp.int32, (16, tail.shape[1]), 0)
    lane = lax.broadcasted_iota(jnp.int32, (16, tail.shape[1]), 1)
    pick_id = jnp.where((sub == lane) & (sub < top), 1.0, 0.0).astype(bf16)
    ids = lax.dot_general(pick_id, tail, (((1,), (1,)), ((), ())), preferred_element_type=f32)
    entry = lax.broadcasted_iota(jnp.int32, ids.shape, 0)
    first = lax.broadcasted_iota(jnp.int32, (rows, rows), 0)
    second = lax.broadcasted_iota(jnp.int32, (rows, rows), 1)
    upper = jnp.where(first <= second, 1.0, 0.0).astype(bf16)
    lower = jnp.where(first >= second, 1.0, 0.0).astype(bf16)
    tail_float = tail.astype(f32)
    tail_lane = lax.broadcasted_iota(jnp.int32, tail.shape, 1)
    slot = lax.broadcasted_iota(jnp.int32, (slots, rows), 0).astype(f32) + 1.0
    slot_lane = lax.broadcasted_iota(jnp.int32, (rows, slots), 1).astype(f32) + 1.0
    named_rows, named_cols = [], []
    for i in range(2):
        expert = experts_ref[0, i].astype(f32)
        hit = jnp.where((ids == expert) & (entry < top), 1.0, 0.0)
        named_rows.append(jnp.sum(hit, axis=0, keepdims=True))
        hit = jnp.where((tail_float == expert) & (tail_lane < top), 1.0, 0.0)
        named_cols.append(jnp.sum(hit, axis=1, keepdims=True))
    stacked = jnp.where(entry < 8, named_rows[0], named_rows[1]).astype(bf16)
    number = jnp.dot(stacked, upper, preferred_element_type=f32)
    pickers = [
        jnp.where((number[8 * i : 8 * i + 1] == slot) & (named_rows[i] > 0.5), 1.0, 0.0) for i in range(2)
    ]
    picker_out[...] = jnp.concatenate(pickers, axis=0).astype(bf16)
    chosen = jnp.dot(picker_out[...], held[...], preferred_element_type=f32).astype(bf16)
    own_out[...] = chosen[:slots]
    mate_out[...] = chosen[slots:]
    wide_lane = lax.broadcasted_iota(jnp.int32, (rows, LANES), 1)
    stacked = jnp.where(wide_lane < LANES // 2, named_cols[0], named_cols[1]).astype(bf16)
    number = jnp.dot(lower, stacked, preferred_element_type=f32)
    placers = [
        jnp.where((number[:, at : at + 1] == slot_lane) & (named > 0.5), 1.0, 0.0)
        for at, named in zip((0, LANES // 2), named_cols)
    ]
    placer_out[...] = jnp.concatenate(placers, axis=1).astype(bf16)


def pick_kernel(count, picker_ref, first_ref, *refs):
    own_out, mate_out, held = refs[count:]
    gather_rows(refs[:count], held)
    rows = jnp.dot(picker_ref[...], held[...], preferred_element_type=jnp.float32).astype(jnp.bfloat16)
    slots, edge = first_ref.shape
    own_out[:, :edge] = first_ref[...]
    own_out[:, edge:] = rows[:slots]
    mate_out[...] = rows[slots:]


def slot_weights(tail, top, expert):
    f32 = jnp.float32
    lane = lax.broadcasted_iota(jnp.int32, tail.shape, 1)
    spare = tail.shape[1]
    first = lax.broadcasted_iota(jnp.int32, (spare, spare), 0)
    second = lax.broadcasted_iota(jnp.int32, (spare, spare), 1)
    shift = jnp.where((first == second + top) & (second < top), 1.0, 0.0).astype(jnp.bfloat16)
    gates = jnp.dot(tail, shift, preferred_element_type=f32)
    hit = (tail.astype(f32) == expert) & (lane < top)
    total = jnp.sum(gates, axis=1, keepdims=True)
    return jnp.sum(jnp.where(hit, gates, 0.0), axis=1, keepdims=True) / jnp.maximum(total, 1.0)


def activate(pre, act, start, end):
    hidden = act.shape[1]
    for at in range(start, end, ACT_COLS):
        to = min(at + ACT_COLS, end)
        gate = pre[:, at:to]
        up = pre[:, hidden + at : hidden + to]
        act[:, at:to] = (gate * jax.nn.sigmoid(1.702 * gate) * (up + 1.0)).astype(act.dtype)


def expert_kernel(
    top, steps_in, spans, experts_ref, own_rows, mate_first, mate_second, win_ref, bias_ref, wout_hbm,
    own_a, mate_a, own_b, mate_b, rows_first, rows_second, pre, act, slot_weight, sems, *held,
):
    step = pl.program_id(0)
    f32, bf16 = jnp.float32, jnp.bfloat16
    slots, hidden, block = mate_first.shape[0], act.shape[1], win_ref.shape[2]
    width = win_ref.shape[1]
    edge = mate_first.shape[1]
    cut = width - mate_second.shape[1]
    early = max((steps_in - 1) * block - hidden, 0) // LANES * LANES
    copies = [
        pltpu.make_async_copy(wout_hbm.at[0, :, pl.ds(at, size)], ref, sems.at[i])
        for i, ((at, size), ref) in enumerate(zip(spans, held))
    ]

    @pl.when(step == 0)
    def _():
        expert = experts_ref[0, 0].astype(f32)
        rows_first[:slots] = own_rows[:, :edge]
        rows_first[slots:] = mate_first[...]
        rows_second[:slots] = own_rows[:, edge:]
        rows_second[slots:] = mate_second[...]
        for i in range(2):
            weight = slot_weights(rows_first[i * slots : (i + 1) * slots, cut:], top, expert)
            slot_weight[i * slots : (i + 1) * slots] = jnp.broadcast_to(weight, (slots, LANES))

    for i, copy in enumerate(copies):

        @pl.when(step == steps_in - (1 if i == 0 else 0))
        def _():
            copy.start()

    def first_layer(at):
        total = jnp.dot(rows_first[:, :cut], win_ref[0, :cut], preferred_element_type=f32)
        total += jnp.dot(rows_second[...], win_ref[0, cut:], preferred_element_type=f32)
        pre[:, pl.ds(at, block)] = total + bias_ref[:, pl.ds(at, block)]

    @pl.when(step < steps_in - 1)
    def _():
        first_layer(pl.multiple_of(step * block, block))

    @pl.when(step == steps_in - 1)
    def _():
        first_layer((steps_in - 1) * block)
        activate(pre, act, 0, early)

    @pl.when(step == steps_in)
    def _():
        activate(pre, act, early, hidden)
        edge = own_a.shape[1]
        for copy, ref, (at, size) in zip(copies, held, spans):
            if at == 0:
                copy.wait()
            elif at == spans[1][0]:
                for later in copies[1:]:
                    later.wait()
            result = jnp.dot(act[:, :early], ref[:early], preferred_element_type=f32)
            result += jnp.dot(act[:, early:], ref[early:], preferred_element_type=f32)
            result = ((result + bias_ref[:, 2 * hidden + at : 2 * hidden + at + size]) * slot_weight[:, :1]).astype(bf16)
            inside = min(max(edge - at, 0), size)
            for row, low, high in ((0, own_a, own_b), (slots, mate_a, mate_b)):
                if inside:
                    low[:, at : at + inside] = result[row : row + slots, :inside]
                if inside < size:
                    high[:, at + inside - edge : at + size - edge] = result[row : row + slots, inside:]
        for ref in (own_b, mate_b):
            ref[:, width - edge :] = jnp.zeros((slots, ref.shape[1] - (width - edge)), bf16)


def spread_kernel(placer_ref, own_ref, mate_ref, *out_refs):
    slots = own_ref.shape[0]
    f32 = jnp.float32
    total = jnp.dot(placer_ref[:, :slots], own_ref[...], preferred_element_type=f32)
    total += jnp.dot(placer_ref[:, slots:], mate_ref[...], preferred_element_type=f32)
    at = 0
    for ref in out_refs:
        ref[...] = total[at : at + ref.shape[0]].astype(ref.dtype)
        at += ref.shape[0]


def params(mib):
    return pltpu.CompilerParams(vmem_limit_bytes=mib * 2**20)


def cost(macs, moved):
    return pl.CostEstimate(flops=2 * macs, bytes_accessed=moved, transcendentals=0)


def ring_shards(tokens, expert_ids, gate_ints, norm_gain, weight_in, bias_in, weight_out, bias_out):
    device_count = lax.axis_size("ep")
    chips = device_count // 2
    reach = chips // 2
    ring = list(range(0, chips, 2)) + list(range(chips - 1, 0, -2))
    right = [(ring[i] * 2 + k, ring[(i + 1) % chips] * 2 + k) for i in range(chips) for k in range(2)]
    left = [(b, a) for a, b in right]
    mate = [(i, i ^ 1) for i in range(device_count)]
    send = lambda value, pairs: lax.ppermute(value, "ep", pairs)
    bf16, f32 = jnp.bfloat16, jnp.float32
    row_count, width = tokens.shape
    top = expert_ids.shape[1]
    hidden = weight_out.shape[1]
    lanes = [2 * BLOCK, width + -width % LANES - 2 * BLOCK]
    cut = width - lanes[1]
    slots, all_rows = chips * CAP, chips * row_count
    vmem = pl.BlockSpec(memory_space=pltpu.VMEM)
    smem = pl.BlockSpec(memory_space=pltpu.SMEM)
    shape = lambda rows, cols, dtype=bf16: jax.ShapeDtypeStruct((rows, cols), dtype)

    chains = pl.pallas_call(
        norm_kernel,
        in_specs=[vmem] * 3,
        out_specs=[vmem] * 2,
        out_shape=[shape(row_count, w) for w in lanes],
        compiler_params=params(NORM_MIB),
    )(tokens, jnp.concatenate([expert_ids.T, gate_ints.T], axis=0), norm_gain)
    me = lax.axis_index("ep").astype(jnp.int32)
    experts = jnp.stack([me, me ^ 1]).reshape(1, 2)
    biases = jnp.concatenate([bias_in, lax.dynamic_slice_in_dim(bias_out, me, 1, axis=0)], axis=1)

    held = [[chain] for chain in chains]
    going = [[chain, chain] for chain in chains]
    for hop in range(1, reach + 1):
        for c in range(len(chains)):
            for way, pairs in enumerate((right, left)):
                if hop < reach or way == c:
                    going[c][way] = send(going[c][way], pairs)
                    held[c].append(going[c][way])
    order = [0]
    for hop in range(1, reach):
        order += [-hop, hop]
    order.append(reach)
    own_first, mate_first, picker, placer = pl.pallas_call(
        functools.partial(route_kernel, top, cut, len(held[0])),
        in_specs=[smem] + [vmem] * len(held[0]),
        out_specs=[vmem] * 4,
        out_shape=[shape(slots, lanes[0])] * 2 + [shape(2 * slots, all_rows), shape(all_rows, 2 * slots)],
        scratch_shapes=[pltpu.VMEM((all_rows, lanes[0]), bf16)],
        cost_estimate=cost(2 * slots * all_rows * lanes[0], 2**20),
        compiler_params=params(PICK_MIB),
    )(experts, *held[0])
    mate_first = send(mate_first, mate)
    own_rows, mate_second = pl.pallas_call(
        functools.partial(pick_kernel, len(held[1])),
        in_specs=[vmem] * (2 + len(held[1])),
        out_specs=[vmem] * 2,
        out_shape=[shape(slots, sum(lanes)), shape(slots, lanes[1])],
        scratch_shapes=[pltpu.VMEM((all_rows, lanes[1]), bf16)],
        cost_estimate=cost(2 * slots * all_rows * lanes[1], 2**20),
        compiler_params=params(PICK_MIB),
    )(picker, own_first, *held[1])
    mate_second = send(mate_second, mate)

    steps_in = pl.cdiv(2 * hidden, COLUMNS)
    spans = [(at, min(COLUMNS, width - at)) for at in range(0, width, COLUMNS)]
    first = lambda j: jnp.minimum(j, steps_in - 1)
    whole = lambda rows, cols: pl.BlockSpec((rows, cols), lambda j: (0, 0), pipeline_mode=pl.Buffered(1))
    own_a, mate_a, own_b, mate_b = pl.pallas_call(
        functools.partial(expert_kernel, top, steps_in, spans),
        grid=(steps_in + 1,),
        in_specs=[
            smem, whole(slots, sum(lanes)), whole(slots, lanes[0]), whole(slots, lanes[1]),
            pl.BlockSpec((1, width, COLUMNS), lambda j: (0, 0, first(j))),
            whole(1, 2 * hidden + width),
            pl.BlockSpec(memory_space=pl.ANY),
        ],
        out_specs=[whole(slots, w) for w in (lanes[0], lanes[0], lanes[1], lanes[1])],
        out_shape=[shape(slots, w) for w in (lanes[0], lanes[0], lanes[1], lanes[1])],
        scratch_shapes=[
            pltpu.VMEM((2 * slots, lanes[0]), bf16),
            pltpu.VMEM((2 * slots, lanes[1]), bf16),
            pltpu.VMEM((2 * slots, steps_in * COLUMNS), f32),
            pltpu.VMEM((2 * slots, hidden), bf16),
            pltpu.VMEM((2 * slots, LANES), f32),
            pltpu.SemaphoreType.DMA((len(spans),)),
        ]
        + [pltpu.VMEM((hidden, size), bf16) for _, size in spans],
        cost_estimate=cost(2 * slots * width * 3 * hidden, 6 * width * hidden),
        compiler_params=params(EXPERT_MIB),
    )(experts, own_rows, mate_first, mate_second, weight_in, biases, weight_out)

    add = lambda a, b: (a.astype(f32) + b.astype(f32)).astype(bf16)
    owed = []
    for own, other in ((own_a, mate_a), (own_b, mate_b)):
        sums = pl.pallas_call(
            spread_kernel,
            in_specs=[vmem] * 3,
            out_specs=[vmem] * chips,
            out_shape=[shape(row_count, own.shape[1])] * chips,
            cost_estimate=cost(2 * slots * all_rows * own.shape[1], 2**20),
            compiler_params=params(SMALL_MIB),
        )(placer, own, send(other, mate))
        owed.append(dict(zip(order, sums)))
    going = [[None, None] for _ in owed]
    for hop in range(reach, 0, -1):
        for c in range(len(owed)):
            for way, pairs in enumerate((right, left)):
                if hop < reach or way == c:
                    mine = owed[c][hop if way == 0 or hop == reach else -hop]
                    passed = mine if going[c][way] is None else add(mine, going[c][way])
                    going[c][way] = send(passed, pairs)
    moe = [o[0].astype(f32) + up.astype(f32) + down.astype(f32) for o, (up, down) in zip(owed, going)]
    return (tokens.astype(f32) + jnp.concatenate(moe, axis=1)[:, :width]).astype(bf16)


def solution(mesh):
    ep = mesh.shape["ep"]

    def shards(*arrays):
        whole_experts = arrays[-1].shape[0] == ep and ep == 16
        return (ring_shards if whole_experts else exchange_shards)(*arrays)

    return jax.shard_map(
        shards,
        mesh=mesh,
        in_specs=(
            P(("groups", "ep"), None),
            P(("groups", "ep"), None),
            P(("groups", "ep"), None),
            P(),
            P("ep", None, None),
            P("ep", None),
            P("ep", None, None),
            P(),
        ),
        out_specs=P(("groups", "ep"), None),
        check_vma=False,
    )
```

```python
import functools

import jax
import jax.numpy as jnp
from jax import lax
from jax.experimental import pallas as pl
from jax.experimental.pallas import tpu as pltpu
from jax.sharding import PartitionSpec as P

CAP = 18
LANES = 128
BLOCK = 768
NORM_MIB = 16
SMALL_MIB = 16
PICK_MIB = 16
EXPERT_MIB = 50
COLUMNS = 1152
ACT_COLS = 256


def route_weights(gate_ints):
    int_gates = gate_ints.astype(jnp.float32)
    return int_gates / jnp.sum(int_gates, axis=1, keepdims=True)


def normalize(tokens, norm_gain):
    tok_float = tokens.astype(jnp.float32)
    row_scale = lax.rsqrt(jnp.mean(tok_float * tok_float, axis=1, keepdims=True) + 1e-05)
    return (tok_float * row_scale * norm_gain[None, :]).astype(jnp.bfloat16)


def exchange_shards(tokens, expert_ids, gate_ints, norm_gain, weight_in, bias_in, weight_out, bias_out):
    device_count = lax.axis_size("ep")
    expert_count = bias_out.shape[0]
    part_count = device_count // expert_count
    row_count, model_width = tokens.shape
    top_count = expert_ids.shape[1]
    capacity = CAP
    tok_float = tokens.astype(jnp.float32)
    normed = normalize(tokens, norm_gain)
    route_weight = route_weights(gate_ints)
    flat_ids = expert_ids.reshape(row_count * top_count)
    one_hot = (flat_ids[:, None] == jnp.arange(expert_count, dtype=jnp.int32)[None, :]).astype(jnp.int32)
    slot_rank = jnp.sum((jnp.cumsum(one_hot, axis=0) - one_hot) * one_hot, axis=1)
    slot_target = (flat_ids * capacity + slot_rank).reshape(row_count, top_count)
    slot_ids = jnp.arange(expert_count * capacity, dtype=jnp.int32)
    slot_match = slot_target[None, :, :] == slot_ids[:, None, None]
    picker = jnp.any(slot_match, axis=2).astype(jnp.bfloat16)
    placed = jnp.dot(picker, normed, preferred_element_type=jnp.float32).astype(jnp.bfloat16)
    combiner = jnp.transpose(jnp.sum(jnp.where(slot_match, route_weight[None, :, :], 0.0), axis=2))
    outgoing = jnp.broadcast_to(
        placed.reshape(expert_count, 1, capacity, model_width),
        (expert_count, part_count, capacity, model_width),
    ).reshape(device_count, capacity, model_width)
    arrived = lax.all_to_all(outgoing, "ep", split_axis=0, concat_axis=0, tiled=True)
    source_count, slot_count = arrived.shape[:2]
    flat_rows = arrived.reshape(source_count * slot_count, model_width)
    pre_act = jnp.dot(flat_rows, weight_in[0], preferred_element_type=jnp.float32) + bias_in[0][None, :]
    half_width = pre_act.shape[1] // 2
    gate_part = pre_act[:, :half_width]
    up_part = pre_act[:, half_width:]
    activated = (gate_part * jax.nn.sigmoid(1.702 * gate_part) * (up_part + 1.0)).astype(jnp.bfloat16)
    result = jnp.dot(activated, weight_out[0], preferred_element_type=jnp.float32).astype(jnp.bfloat16)
    returned = lax.all_to_all(
        result.reshape(source_count, slot_count, model_width), "ep", split_axis=0, concat_axis=0, tiled=True
    )
    part_sum = jnp.sum(
        returned.reshape(expert_count, part_count, capacity, model_width), axis=1, dtype=jnp.float32
    ).reshape(expert_count * capacity, model_width)
    moe_rows = jnp.dot(combiner, part_sum, precision=lax.Precision.HIGHEST)
    expert_hot = expert_ids[:, :, None] == jnp.arange(expert_count, dtype=jnp.int32)[None, None, :]
    expert_weight = jnp.sum(jnp.where(expert_hot, route_weight[:, :, None], 0.0), axis=1)
    bias_term = jnp.dot(expert_weight, bias_out, precision=lax.Precision.HIGHEST)
    return (tok_float + moe_rows + bias_term).astype(jnp.bfloat16)


def norm_kernel(tokens_ref, named_ref, gain_ref, first_ref, second_ref):
    f32, bf16 = jnp.float32, jnp.bfloat16
    tok = tokens_ref[...].astype(f32)
    scale = lax.rsqrt(jnp.mean(tok * tok, axis=1, keepdims=True) + 1e-05)
    normed = (tok * scale * gain_ref[...][None, :]).astype(bf16)
    cut = tok.shape[1] - second_ref.shape[1]
    spare = first_ref.shape[1] - cut
    entries = named_ref.shape[0]
    sub = lax.broadcasted_iota(jnp.int32, (entries, spare), 0)
    lane = lax.broadcasted_iota(jnp.int32, (entries, spare), 1)
    tail = lax.dot_general(
        named_ref[...].astype(f32),
        jnp.where(lane == sub, 1.0, 0.0),
        (((0,), (0,)), ((), ())),
        preferred_element_type=f32,
    )
    first_ref[:, :cut] = normed[:, :cut]
    first_ref[:, cut:] = tail.astype(bf16)
    second_ref[...] = normed[:, cut:]


def gather_rows(pieces, held):
    at = 0
    for ref in pieces:
        held[at : at + ref.shape[0]] = ref[...]
        at += ref.shape[0]


def route_kernel(top, cut, count, experts_ref, *refs):
    f32, bf16 = jnp.float32, jnp.bfloat16
    own_out, mate_out, picker_out, placer_out, held = refs[count:]
    gather_rows(refs[:count], held)
    tail = held[:, cut:]
    slots = own_out.shape[0]
    rows = tail.shape[0]
    sub = lax.broadcasted_iota(jnp.int32, (16, tail.shape[1]), 0)
    lane = lax.broadcasted_iota(jnp.int32, (16, tail.shape[1]), 1)
    pick_id = jnp.where((sub == lane) & (sub < top), 1.0, 0.0).astype(bf16)
    ids = lax.dot_general(pick_id, tail, (((1,), (1,)), ((), ())), preferred_element_type=f32)
    entry = lax.broadcasted_iota(jnp.int32, ids.shape, 0)
    first = lax.broadcasted_iota(jnp.int32, (rows, rows), 0)
    second = lax.broadcasted_iota(jnp.int32, (rows, rows), 1)
    upper = jnp.where(first <= second, 1.0, 0.0).astype(bf16)
    lower = jnp.where(first >= second, 1.0, 0.0).astype(bf16)
    tail_float = tail.astype(f32)
    tail_lane = lax.broadcasted_iota(jnp.int32, tail.shape, 1)
    slot = lax.broadcasted_iota(jnp.int32, (slots, rows), 0).astype(f32) + 1.0
    slot_lane = lax.broadcasted_iota(jnp.int32, (rows, slots), 1).astype(f32) + 1.0
    named_rows, named_cols = [], []
    for i in range(2):
        expert = experts_ref[0, i].astype(f32)
        hit = jnp.where((ids == expert) & (entry < top), 1.0, 0.0)
        named_rows.append(jnp.sum(hit, axis=0, keepdims=True))
        hit = jnp.where((tail_float == expert) & (tail_lane < top), 1.0, 0.0)
        named_cols.append(jnp.sum(hit, axis=1, keepdims=True))
    stacked = jnp.where(entry < 8, named_rows[0], named_rows[1]).astype(bf16)
    number = jnp.dot(stacked, upper, preferred_element_type=f32)
    pickers = [
        jnp.where((number[8 * i : 8 * i + 1] == slot) & (named_rows[i] > 0.5), 1.0, 0.0) for i in range(2)
    ]
    picker_out[...] = jnp.concatenate(pickers, axis=0).astype(bf16)
    chosen = jnp.dot(picker_out[...], held[...], preferred_element_type=f32).astype(bf16)
    own_out[...] = chosen[:slots]
    mate_out[...] = chosen[slots:]
    wide_lane = lax.broadcasted_iota(jnp.int32, (rows, LANES), 1)
    stacked = jnp.where(wide_lane < LANES // 2, named_cols[0], named_cols[1]).astype(bf16)
    number = jnp.dot(lower, stacked, preferred_element_type=f32)
    placers = [
        jnp.where((number[:, at : at + 1] == slot_lane) & (named > 0.5), 1.0, 0.0)
        for at, named in zip((0, LANES // 2), named_cols)
    ]
    placer_out[...] = jnp.concatenate(placers, axis=1).astype(bf16)


def pick_kernel(count, picker_ref, first_ref, *refs):
    own_out, mate_out, held = refs[count:]
    gather_rows(refs[:count], held)
    rows = jnp.dot(picker_ref[...], held[...], preferred_element_type=jnp.float32).astype(jnp.bfloat16)
    slots, edge = first_ref.shape
    own_out[:, :edge] = first_ref[...]
    own_out[:, edge:] = rows[:slots]
    mate_out[...] = rows[slots:]


def slot_weights(tail, top, expert):
    f32 = jnp.float32
    lane = lax.broadcasted_iota(jnp.int32, tail.shape, 1)
    spare = tail.shape[1]
    first = lax.broadcasted_iota(jnp.int32, (spare, spare), 0)
    second = lax.broadcasted_iota(jnp.int32, (spare, spare), 1)
    shift = jnp.where((first == second + top) & (second < top), 1.0, 0.0).astype(jnp.bfloat16)
    gates = jnp.dot(tail, shift, preferred_element_type=f32)
    hit = (tail.astype(f32) == expert) & (lane < top)
    total = jnp.sum(gates, axis=1, keepdims=True)
    return jnp.sum(jnp.where(hit, gates, 0.0), axis=1, keepdims=True) / jnp.maximum(total, 1.0)


def activate(pre, act, start, end):
    hidden = act.shape[1]
    for at in range(start, end, ACT_COLS):
        to = min(at + ACT_COLS, end)
        gate = pre[:, at:to]
        up = pre[:, hidden + at : hidden + to]
        act[:, at:to] = (gate * jax.nn.sigmoid(1.702 * gate) * (up + 1.0)).astype(act.dtype)


def expert_kernel(
    top, steps_in, spans, experts_ref, own_rows, mate_first, mate_second, win_ref, bias_ref, wout_hbm,
    own_a, mate_a, own_b, mate_b, rows_first, rows_second, pre, act, slot_weight, sems, *held,
):
    step = pl.program_id(0)
    f32, bf16 = jnp.float32, jnp.bfloat16
    slots, hidden, block = mate_first.shape[0], act.shape[1], win_ref.shape[2]
    width = win_ref.shape[1]
    edge = mate_first.shape[1]
    cut = width - mate_second.shape[1]
    early = max((steps_in - 1) * block - hidden, 0) // LANES * LANES
    copies = [
        pltpu.make_async_copy(wout_hbm.at[0, :, pl.ds(at, size)], ref, sems.at[i])
        for i, ((at, size), ref) in enumerate(zip(spans, held))
    ]

    @pl.when(step == 0)
    def _():
        expert = experts_ref[0, 0].astype(f32)
        rows_first[:slots] = own_rows[:, :edge]
        rows_first[slots:] = mate_first[...]
        rows_second[:slots] = own_rows[:, edge:]
        rows_second[slots:] = mate_second[...]
        for i in range(2):
            weight = slot_weights(rows_first[i * slots : (i + 1) * slots, cut:], top, expert)
            slot_weight[i * slots : (i + 1) * slots] = jnp.broadcast_to(weight, (slots, LANES))

    for i, copy in enumerate(copies):

        @pl.when(step == steps_in - (1 if i == 0 else 0))
        def _():
            copy.start()

    def first_layer(at):
        total = jnp.dot(rows_first[:, :cut], win_ref[0, :cut], preferred_element_type=f32)
        total += jnp.dot(rows_second[...], win_ref[0, cut:], preferred_element_type=f32)
        pre[:, pl.ds(at, block)] = total + bias_ref[:, pl.ds(at, block)]

    @pl.when(step < steps_in - 1)
    def _():
        first_layer(pl.multiple_of(step * block, block))

    @pl.when(step == steps_in - 1)
    def _():
        first_layer((steps_in - 1) * block)
        activate(pre, act, 0, early)

    @pl.when(step == steps_in)
    def _():
        activate(pre, act, early, hidden)
        edge = own_a.shape[1]
        for copy, ref, (at, size) in zip(copies, held, spans):
            if at == 0:
                copy.wait()
            elif at == spans[1][0]:
                for later in copies[1:]:
                    later.wait()
            result = jnp.dot(act[:, :early], ref[:early], preferred_element_type=f32)
            result += jnp.dot(act[:, early:], ref[early:], preferred_element_type=f32)
            result = ((result + bias_ref[:, 2 * hidden + at : 2 * hidden + at + size]) * slot_weight[:, :1]).astype(bf16)
            inside = min(max(edge - at, 0), size)
            for row, low, high in ((0, own_a, own_b), (slots, mate_a, mate_b)):
                if inside:
                    low[:, at : at + inside] = result[row : row + slots, :inside]
                if inside < size:
                    high[:, at + inside - edge : at + size - edge] = result[row : row + slots, inside:]
        for ref in (own_b, mate_b):
            ref[:, width - edge :] = jnp.zeros((slots, ref.shape[1] - (width - edge)), bf16)


def spread_kernel(placer_ref, own_ref, mate_ref, *out_refs):
    slots = own_ref.shape[0]
    f32 = jnp.float32
    total = jnp.dot(placer_ref[:, :slots], own_ref[...], preferred_element_type=f32)
    total += jnp.dot(placer_ref[:, slots:], mate_ref[...], preferred_element_type=f32)
    at = 0
    for ref in out_refs:
        ref[...] = total[at : at + ref.shape[0]].astype(ref.dtype)
        at += ref.shape[0]


def params(mib):
    return pltpu.CompilerParams(vmem_limit_bytes=mib * 2**20)


def cost(macs, moved):
    return pl.CostEstimate(flops=2 * macs, bytes_accessed=moved, transcendentals=0)


def ring_shards(tokens, expert_ids, gate_ints, norm_gain, weight_in, bias_in, weight_out, bias_out):
    device_count = lax.axis_size("ep")
    chips = device_count // 2
    reach = chips // 2
    ring = list(range(0, chips, 2)) + list(range(chips - 1, 0, -2))
    right = [(ring[i] * 2 + k, ring[(i + 1) % chips] * 2 + k) for i in range(chips) for k in range(2)]
    left = [(b, a) for a, b in right]
    mate = [(i, i ^ 1) for i in range(device_count)]
    send = lambda value, pairs: lax.ppermute(value, "ep", pairs)
    bf16, f32 = jnp.bfloat16, jnp.float32
    row_count, width = tokens.shape
    top = expert_ids.shape[1]
    hidden = weight_out.shape[1]
    lanes = [2 * BLOCK, width + -width % LANES - 2 * BLOCK]
    cut = width - lanes[1]
    slots, all_rows = chips * CAP, chips * row_count
    vmem = pl.BlockSpec(memory_space=pltpu.VMEM)
    smem = pl.BlockSpec(memory_space=pltpu.SMEM)
    shape = lambda rows, cols, dtype=bf16: jax.ShapeDtypeStruct((rows, cols), dtype)

    chains = pl.pallas_call(
        norm_kernel,
        in_specs=[vmem] * 3,
        out_specs=[vmem] * 2,
        out_shape=[shape(row_count, w) for w in lanes],
        compiler_params=params(NORM_MIB),
    )(tokens, jnp.concatenate([expert_ids.T, gate_ints.T], axis=0), norm_gain)
    me = lax.axis_index("ep").astype(jnp.int32)
    experts = jnp.stack([me, me ^ 1]).reshape(1, 2)
    biases = jnp.concatenate([bias_in, lax.dynamic_slice_in_dim(bias_out, me, 1, axis=0)], axis=1)

    held = [[chain] for chain in chains]
    going = [[chain, chain] for chain in chains]
    for hop in range(1, reach + 1):
        for c in range(len(chains)):
            for way, pairs in enumerate((right, left)):
                if hop < reach or way == c:
                    going[c][way] = send(going[c][way], pairs)
                    held[c].append(going[c][way])
    held[0][-1], biases = lax.optimization_barrier((held[0][-1], biases))
    order = [0]
    for hop in range(1, reach):
        order += [-hop, hop]
    order.append(reach)
    own_first, mate_first, picker, placer = pl.pallas_call(
        functools.partial(route_kernel, top, cut, len(held[0])),
        in_specs=[smem] + [vmem] * len(held[0]),
        out_specs=[vmem] * 4,
        out_shape=[shape(slots, lanes[0])] * 2 + [shape(2 * slots, all_rows), shape(all_rows, 2 * slots)],
        scratch_shapes=[pltpu.VMEM((all_rows, lanes[0]), bf16)],
        cost_estimate=cost(2 * slots * all_rows * lanes[0], 2**20),
        compiler_params=params(PICK_MIB),
    )(experts, *held[0])
    mate_first = send(mate_first, mate)
    own_rows, mate_second = pl.pallas_call(
        functools.partial(pick_kernel, len(held[1])),
        in_specs=[vmem] * (2 + len(held[1])),
        out_specs=[vmem] * 2,
        out_shape=[shape(slots, sum(lanes)), shape(slots, lanes[1])],
        scratch_shapes=[pltpu.VMEM((all_rows, lanes[1]), bf16)],
        cost_estimate=cost(2 * slots * all_rows * lanes[1], 2**20),
        compiler_params=params(PICK_MIB),
    )(picker, own_first, *held[1])
    mate_second = send(mate_second, mate)

    steps_in = pl.cdiv(2 * hidden, COLUMNS)
    spans = [(at, min(COLUMNS, width - at)) for at in range(0, width, COLUMNS)]
    first = lambda j: jnp.minimum(j, steps_in - 1)
    whole = lambda rows, cols: pl.BlockSpec((rows, cols), lambda j: (0, 0), pipeline_mode=pl.Buffered(1))
    own_a, mate_a, own_b, mate_b = pl.pallas_call(
        functools.partial(expert_kernel, top, steps_in, spans),
        grid=(steps_in + 1,),
        in_specs=[
            smem, whole(slots, sum(lanes)), whole(slots, lanes[0]), whole(slots, lanes[1]),
            pl.BlockSpec((1, width, COLUMNS), lambda j: (0, 0, first(j))),
            whole(1, 2 * hidden + width),
            pl.BlockSpec(memory_space=pl.ANY),
        ],
        out_specs=[whole(slots, w) for w in (lanes[0], lanes[0], lanes[1], lanes[1])],
        out_shape=[shape(slots, w) for w in (lanes[0], lanes[0], lanes[1], lanes[1])],
        scratch_shapes=[
            pltpu.VMEM((2 * slots, lanes[0]), bf16),
            pltpu.VMEM((2 * slots, lanes[1]), bf16),
            pltpu.VMEM((2 * slots, steps_in * COLUMNS), f32),
            pltpu.VMEM((2 * slots, hidden), bf16),
            pltpu.VMEM((2 * slots, LANES), f32),
            pltpu.SemaphoreType.DMA((len(spans),)),
        ]
        + [pltpu.VMEM((hidden, size), bf16) for _, size in spans],
        cost_estimate=cost(2 * slots * width * 3 * hidden, 6 * width * hidden),
        compiler_params=params(EXPERT_MIB),
    )(experts, own_rows, mate_first, mate_second, weight_in, biases, weight_out)

    add = lambda a, b: (a.astype(f32) + b.astype(f32)).astype(bf16)
    owed = []
    for own, other in ((own_a, mate_a), (own_b, mate_b)):
        sums = pl.pallas_call(
            spread_kernel,
            in_specs=[vmem] * 3,
            out_specs=[vmem] * chips,
            out_shape=[shape(row_count, own.shape[1])] * chips,
            cost_estimate=cost(2 * slots * all_rows * own.shape[1], 2**20),
            compiler_params=params(SMALL_MIB),
        )(placer, own, send(other, mate))
        owed.append(dict(zip(order, sums)))
    going = [[None, None] for _ in owed]
    for hop in range(reach, 0, -1):
        for c in range(len(owed)):
            for way, pairs in enumerate((right, left)):
                if hop < reach or way == c:
                    mine = owed[c][hop if way == 0 or hop == reach else -hop]
                    passed = mine if going[c][way] is None else add(mine, going[c][way])
                    going[c][way] = send(passed, pairs)
    moe = [o[0].astype(f32) + up.astype(f32) + down.astype(f32) for o, (up, down) in zip(owed, going)]
    return (tokens.astype(f32) + jnp.concatenate(moe, axis=1)[:, :width]).astype(bf16)


def solution(mesh):
    ep = mesh.shape["ep"]

    def shards(*arrays):
        whole_experts = arrays[-1].shape[0] == ep and ep == 16
        return (ring_shards if whole_experts else exchange_shards)(*arrays)

    return jax.shard_map(
        shards,
        mesh=mesh,
        in_specs=(
            P(("groups", "ep"), None),
            P(("groups", "ep"), None),
            P(("groups", "ep"), None),
            P(),
            P("ep", None, None),
            P("ep", None),
            P("ep", None, None),
            P(),
        ),
        out_specs=P(("groups", "ep"), None),
        check_vma=False,
    )
```
